32 devices in a mesh: dp: 4 (over y, x), space: 8 (over z, core).
Axes of the slice: x: 2, y: 2, z: 4, core: 2. Of those that a mesh axis runs over, the one named last changes fastest.
Arguments:
- fields: bfloat16 [4, 32, 768, 128], P('dp', None, 'space'), may hold values from -6 to 6
- land_mask: int32 [768, 128], P('space'), may hold values from 0 to 1, as said below
- land_frac: float32 [768, 128], P('space'), may hold values from 0.05 to 1
- owner_map: int32 [1536], replicated, may hold values from 0 to 1535, as said below
- targets: float32 [4, 14, 1536], P('dp', None, 'space'), may hold values from -3 to 3
- conv_weight: bfloat16 [3, 3, 32, 128], replicated, may hold values from -0.375 to 0.375
- conv_bias: float32 [128], replicated, may hold values from -3 to 3
- mix_weight: bfloat16 [128, 128], replicated, may hold values from -0.5 to 0.5
- mix_bias: float32 [128], replicated, may hold values from -3 to 3
- out_weight: bfloat16 [128, 14], replicated, may hold values from -0.5 to 0.5
- out_bias: float32 [14], replicated, may hold values from -3 to 3
Outputs:
- coarse_pred: float32 [4, 14, 1536], P('dp', None, 'space')
- conv_grad: float32 [3, 3, 32, 128], replicated
- conv_bias_grad: float32 [128], replicated
- mix_grad: float32 [128, 128], replicated
- mix_bias_grad: float32 [128], replicated
- out_grad: float32 [128, 14], replicated
- out_bias_grad: float32 [14], replicated
- loss: float32 [], replicated
The draws below stay inside these ranges and needn't reach their ends.
Inputs may be any that keep to these rules, and one draw needn't show every extreme that they name: A permutation. Coarse cell g is owned by index owner_map[g] // 192 of space, at local place owner_map[g] % 192; the 192 coarse cells of every strip go to every owner exactly 24 at a time. `land_mask`: 1 marks land.
All inputs are finite; a program needn't handle non-finite values.
Results may differ from the reference program's by a relative error of at most 0.00039.
Values may be sent and summed in bfloat16 or wider, within the bound.
No kernel may reach another device: no remote copies, remote signals or barrier semaphores. Data moves between devices by JAX's collectives and lax.ppermute only.
A program may use at most 128 MiB of HBM per device.

```python
import math
import jax
import jax.numpy as jnp
from jax import lax

WIDTH = 128
POOLS = 14
CHANNELS = 32
SIDE = 8
ROWS = 96
COLUMNS = 128
MEMBERS = 4
ALL_ROWS = 768
BLOCKS = 192
COARSE = 1536
CAPACITY = 24
N_SPACE = 8


def draw_owner_map(key, part):
    strip_keys = jax.random.split(jax.random.fold_in(key, 11), N_SPACE)
    shuffled = jax.vmap(lambda single: jax.random.permutation(single, BLOCKS))(strip_keys)
    owners = (shuffled // CAPACITY).reshape(-1).astype(jnp.int32)
    breakers = jax.random.permutation(jax.random.fold_in(key, 12), COARSE).astype(jnp.int32)
    places = jnp.argsort(owners * COARSE + breakers)
    return jnp.zeros((COARSE,), jnp.int32).at[places].set(jnp.arange(COARSE, dtype=jnp.int32))


def draw_land_mask(key, part):
    share = jax.random.randint(jax.random.fold_in(key, 21), (ALL_ROWS // SIDE, COLUMNS // SIDE), 0, SIDE * SIDE + 1)
    picks = jax.random.randint(jax.random.fold_in(key, 22), (ALL_ROWS, COLUMNS), 0, SIDE * SIDE)
    share_cells = jnp.repeat(jnp.repeat(share, SIDE, axis=0), SIDE, axis=1)
    return (picks < share_cells).astype(jnp.int32)


def shard_levels(rng, shape, cuts, low, top_value):
    factor_of = 1.0
    for position, blocks in cuts:
        draws = jax.random.uniform(jax.random.fold_in(jax.random.fold_in(rng, 6), position), (blocks,), jnp.float32, low / len(cuts), top_value / len(cuts))
        factor_of = factor_of * jnp.repeat(jnp.exp(draws), shape[position] // blocks).reshape((-1,) + (1,) * (len(shape) - 1 - position))
    return factor_of


def normal_values(rng, extent, deviation, most, cuts=(), kind=jnp.bfloat16):
    array = jax.random.normal(rng, extent, jnp.float32) * deviation
    if len(cuts) > 0:
        array = shard_levels(rng, extent, cuts, -0.22, 0.18) * array
    return jnp.clip(array, min=-most, max=most).astype(kind)


def setup_inputs(seed: int = 0) -> dict:
    splits = jax.random.split(jax.random.key(seed), 12)
    fields = normal_values(splits[0], (MEMBERS, CHANNELS, ALL_ROWS, COLUMNS), 1.0, 6.0, ((0, 4), (2, 8)))
    land_mask = draw_land_mask(jax.random.fold_in(splits[11], 71), 0)
    land_frac = jnp.clip(0.05 + 0.95 * jax.random.uniform(splits[2], (ALL_ROWS, COLUMNS), jnp.float32) ** shard_levels(splits[2], (ALL_ROWS, COLUMNS), ((0, 8),), -0.2, 0.2), 0.05, 1.0)
    owner_map = draw_owner_map(jax.random.fold_in(splits[11], 71), 0)
    targets = normal_values(splits[4], (MEMBERS, POOLS, COARSE), 0.5, 3.0, ((0, 4), (2, 8)), jnp.float32)
    conv_weight = normal_values(splits[5], (3, 3, CHANNELS, WIDTH), (9 * CHANNELS) ** -0.5, 0.375)
    conv_bias = normal_values(splits[6], (WIDTH,), 0.5, 3.0, (), jnp.float32)
    mix_weight = normal_values(splits[7], (WIDTH, WIDTH), WIDTH ** -0.5, 0.5)
    mix_bias = normal_values(splits[8], (WIDTH,), 0.5, 3.0, (), jnp.float32)
    out_weight = normal_values(splits[9], (WIDTH, POOLS), WIDTH ** -0.5, 0.5)
    out_bias = normal_values(splits[10], (POOLS,), 0.5, 3.0, (), jnp.float32)
    return dict(fields=fields, land_mask=land_mask, land_frac=land_frac, owner_map=owner_map, targets=targets, conv_weight=conv_weight, conv_bias=conv_bias, mix_weight=mix_weight, mix_bias=mix_bias, out_weight=out_weight, out_bias=out_bias)


CUBIC = 0.044715
ROOT_TWO_PI = math.sqrt(2.0 / math.pi)

def gelu_pair(pre):
    inner = ROOT_TWO_PI * (pre + CUBIC * pre * pre * pre)
    tanh_value = jnp.tanh(inner)
    value = 0.5 * pre * (1.0 + tanh_value)
    slope = 0.5 * (1.0 + tanh_value) + 0.5 * pre * (1.0 - tanh_value * tanh_value) * ROOT_TWO_PI * (1.0 + 3.0 * CUBIC * pre * pre)
    return (value, slope)

def product(form, left, right):
    return jnp.einsum(form, left.astype(jnp.float32), right.astype(jnp.float32))

def block_sums(values, side):
    leading = values.shape[:-2]
    height, breadth = (values.shape[-2], values.shape[-1])
    shaped = values.reshape(leading + (height // side, side, breadth // side, side))
    return lax.optimization_barrier(jnp.sum(shaped, axis=(-3, -1))).reshape(leading + (height // side * (breadth // side),))

def forward_tile(padded, conv_weight, conv_bias, mix_weight, mix_bias, out_weight, out_bias):
    height = padded.shape[2] - 2
    breadth = padded.shape[3] - 2
    pieces = [padded[:, :, row_shift:row_shift + height, col_shift:col_shift + breadth] for row_shift in range(3) for col_shift in range(3)]
    stacked = jnp.concatenate(pieces, axis=1)
    flat_weight = conv_weight.reshape(-1, conv_weight.shape[3])
    pre_one = product('mkrc,kh->mrch', stacked, flat_weight) + conv_bias
    value_one, slope_one = gelu_pair(pre_one)
    hidden_one = value_one.astype(jnp.bfloat16)
    pre_two = product('mrch,hg->mrcg', hidden_one, mix_weight) + mix_bias
    value_two, slope_two = gelu_pair(pre_two)
    hidden_two = value_two.astype(jnp.bfloat16)
    raw = product('mrch,hp->mprc', hidden_two, out_weight) + out_bias[None, :, None, None]
    return (stacked, slope_one, hidden_one, slope_two, hidden_two, raw)

def backward_tile(stacked, slope_one, hidden_one, slope_two, hidden_two, raw, weight_map, d_block, mix_weight, out_weight, side):
    members, pools = (d_block.shape[0], d_block.shape[1])
    height, breadth = weight_map.shape
    d_cells = d_block.reshape(members, pools, height // side, breadth // side)
    d_cells = jnp.repeat(jnp.repeat(d_cells, side, axis=2), side, axis=3)
    d_raw = (d_cells * weight_map * jax.nn.sigmoid(raw)).astype(jnp.bfloat16)
    out_grad = product('mrch,mprc->hp', hidden_two, d_raw)
    out_bias_grad = lax.optimization_barrier(jnp.sum(d_raw.astype(jnp.float32), axis=(0, 2, 3)))
    d_two = (product('mprc,hp->mrch', d_raw, out_weight) * slope_two).astype(jnp.bfloat16)
    mix_grad = product('mrch,mrcg->hg', hidden_one, d_two)
    mix_bias_grad = lax.optimization_barrier(jnp.sum(d_two.astype(jnp.float32), axis=(0, 1, 2)))
    d_one = (product('mrcg,hg->mrch', d_two, mix_weight) * slope_one).astype(jnp.bfloat16)
    conv_grad = product('mkrc,mrch->kh', stacked, d_one)
    conv_bias_grad = lax.optimization_barrier(jnp.sum(d_one.astype(jnp.float32), axis=(0, 1, 2)))
    return (conv_grad, conv_bias_grad, mix_grad, mix_bias_grad, out_grad, out_bias_grad)

def reference(fields, land_mask, land_frac, owner_map, targets, conv_weight, conv_bias, mix_weight, mix_bias, out_weight, out_bias):
    padded_all = jnp.pad(fields, ((0, 0), (0, 0), (1, 1), (1, 1)))
    weight_all = land_frac * land_mask.astype(jnp.float32)
    tiles = MEMBERS * N_SPACE
    zero = jnp.zeros((), jnp.int32)

    def tile_inputs(serial):
        member = (serial // N_SPACE).astype(jnp.int32)
        strip = (serial % N_SPACE).astype(jnp.int32)
        slab = lax.dynamic_slice(padded_all, (member, zero, strip * ROWS, zero), (1, CHANNELS, ROWS + 2, COLUMNS + 2))
        weight_map = lax.dynamic_slice(weight_all, (strip * ROWS, zero), (ROWS, COLUMNS))
        return (member, strip, slab, weight_map)

    def first_pass(serial):
        member, strip, slab, weight_map = tile_inputs(serial)
        outputs = forward_tile(slab, conv_weight, conv_bias, mix_weight, mix_bias, out_weight, out_bias)
        density = jax.nn.softplus(outputs[5]) * weight_map
        return block_sums(density, SIDE)[0]
    serials = jnp.arange(tiles, dtype=jnp.int32)
    sums = lax.map(first_pass, serials)
    sums = sums.reshape(MEMBERS, N_SPACE, POOLS, BLOCKS).transpose(0, 2, 1, 3).reshape(MEMBERS, POOLS, COARSE)
    denom_global = jnp.maximum(block_sums(weight_all, SIDE), 1.0)
    coarse_global = sums / denom_global
    coarse_pred = jnp.zeros((MEMBERS, POOLS, COARSE), jnp.float32).at[:, :, owner_map].set(coarse_global)
    residual_global = coarse_global - targets[:, :, owner_map]
    count_all = MEMBERS * POOLS * COARSE
    loss = 0.5 * jnp.sum(residual_global * residual_global) / count_all
    d_global = residual_global / (math.sqrt(count_all) * denom_global)

    def second_pass(carry, serial):
        member, strip, slab, weight_map = tile_inputs(serial)
        outputs = forward_tile(slab, conv_weight, conv_bias, mix_weight, mix_bias, out_weight, out_bias)
        d_block = lax.dynamic_slice(d_global, (member, zero, strip * BLOCKS), (1, POOLS, BLOCKS))
        grads = backward_tile(*outputs, weight_map, d_block, mix_weight, out_weight, SIDE)
        return (tuple((first + second for first, second in zip(carry, grads))), None)
    initial = (jnp.zeros((9 * CHANNELS, WIDTH), jnp.float32), jnp.zeros((WIDTH,), jnp.float32), jnp.zeros((WIDTH, WIDTH), jnp.float32), jnp.zeros((WIDTH,), jnp.float32), jnp.zeros((WIDTH, POOLS), jnp.float32), jnp.zeros((POOLS,), jnp.float32))
    grads, _ = lax.scan(second_pass, initial, serials)
    conv_grad = grads[0].reshape(3, 3, CHANNELS, WIDTH)
    return (coarse_pred, conv_grad, grads[1], grads[2], grads[3], grads[4], grads[5], loss)
```

```python
import math

import jax
import jax.numpy as jnp
from jax import lax
from jax.sharding import PartitionSpec as P

SIDE = 8


CUBIC = 0.044715
ROOT_TWO_PI = math.sqrt(2.0 / math.pi)


def padded_2(block, sides, width):
    for axis, dim in sides:
        count = lax.axis_size(axis)
        forward = [(i, i + 1) for i in range(count - 1)]
        backward = [(target, source) for source, target in forward]
        low = lax.ppermute(
            lax.slice_in_dim(block, block.shape[dim] - width, None, axis=dim), axis, forward
        )
        high = lax.ppermute(lax.slice_in_dim(block, 0, width, axis=dim), axis, backward)
        block = jnp.concatenate([low, block, high], axis=dim)
    return block


def gelu_pair(pre):
    inner = ROOT_TWO_PI * (pre + CUBIC * pre * pre * pre)
    tanh_value = jnp.tanh(inner)
    value = 0.5 * pre * (1.0 + tanh_value)
    slope = 0.5 * (1.0 + tanh_value) + 0.5 * pre * (1.0 - tanh_value * tanh_value) * ROOT_TWO_PI * (
        1.0 + 3.0 * CUBIC * pre * pre
    )
    return (value, slope)


def product(form, left, right):
    return jnp.einsum(form, left, right, preferred_element_type=jnp.float32)


def block_sums(values, side):
    leading = values.shape[:-2]
    height, breadth = (values.shape[-2], values.shape[-1])
    shaped = values.reshape(leading + (height // side, side, breadth // side, side))
    return jnp.sum(shaped, axis=(-3, -1)).reshape(leading + (height // side * (breadth // side),))


def forward_tile(padded, conv_weight, conv_bias, mix_weight, mix_bias, out_weight, out_bias):
    height = padded.shape[2] - 2
    breadth = padded.shape[3] - 2
    pieces = [
        padded[:, :, row_shift : row_shift + height, col_shift : col_shift + breadth]
        for row_shift in range(3)
        for col_shift in range(3)
    ]
    stacked = jnp.concatenate(pieces, axis=1)
    flat_weight = conv_weight.reshape(-1, conv_weight.shape[3])
    pre_one = product("mkrc,kh->mrch", stacked, flat_weight) + conv_bias
    value_one, slope_one = gelu_pair(pre_one)
    hidden_one = value_one.astype(jnp.bfloat16)
    pre_two = product("mrch,hg->mrcg", hidden_one, mix_weight) + mix_bias
    value_two, slope_two = gelu_pair(pre_two)
    hidden_two = value_two.astype(jnp.bfloat16)
    raw = product("mrch,hp->mprc", hidden_two, out_weight) + out_bias[None, :, None, None]
    return (stacked, slope_one, hidden_one, slope_two, hidden_two, raw)


def backward_tile(
    stacked,
    slope_one,
    hidden_one,
    slope_two,
    hidden_two,
    raw,
    weight_map,
    d_block,
    mix_weight,
    out_weight,
    side,
):
    members, pools = (d_block.shape[0], d_block.shape[1])
    height, breadth = weight_map.shape
    d_cells = d_block.reshape(members, pools, height // side, breadth // side)
    d_cells = jnp.repeat(jnp.repeat(d_cells, side, axis=2), side, axis=3)
    d_raw = (d_cells * weight_map * jax.nn.sigmoid(raw)).astype(jnp.bfloat16)
    out_grad = product("mrch,mprc->hp", hidden_two, d_raw)
    out_bias_grad = jnp.sum(d_raw.astype(jnp.float32), axis=(0, 2, 3))
    d_two = (product("mprc,hp->mrch", d_raw, out_weight) * slope_two).astype(jnp.bfloat16)
    mix_grad = product("mrch,mrcg->hg", hidden_one, d_two)
    mix_bias_grad = jnp.sum(d_two.astype(jnp.float32), axis=(0, 1, 2))
    d_one = (product("mrcg,hg->mrch", d_two, mix_weight) * slope_one).astype(jnp.bfloat16)
    conv_grad = product("mkrc,mrch->kh", stacked, d_one)
    conv_bias_grad = jnp.sum(d_one.astype(jnp.float32), axis=(0, 1, 2))
    return (conv_grad, conv_bias_grad, mix_grad, mix_bias_grad, out_grad, out_bias_grad)


def bits_of(size, low):
    return [1 << k for k in range(size.bit_length() - 1) if (1 << k) >= low]


def swapped(values, axis, bit):
    return lax.ppermute(values, axis, [(i, i ^ bit) for i in range(lax.axis_size(axis))])


def gather_relative(values, axis, bits):
    for bit in bits:
        values = jnp.concatenate([values, swapped(values, axis, bit)], axis=0)
    return values


def crossed(values, step):
    dp, space = lax.axis_size("dp"), lax.axis_size("space")
    dp_moves = [(bit, 0) for bit in bits_of(dp, 1)]
    space_moves = [(0, bit) for bit in bits_of(space, 2)]
    orders = (dp_moves + space_moves, space_moves + dp_moves)
    pairs = []
    for d in range(dp):
        for s in range(space):
            d_bit, s_bit = orders[s % 2][step]
            pairs.append((d * space + s, (d ^ d_bit) * space + (s ^ s_bit)))
    return lax.ppermute(values, ("dp", "space"), pairs)


def reduce_all(keep, send, coarse):
    space = lax.axis_size("space")
    n_dp, n_space = len(bits_of(lax.axis_size("dp"), 1)), len(bits_of(space, 2))
    core = lax.axis_index("space") % 2
    rows = keep.shape[0]
    got = swapped(jnp.concatenate([send, coarse], axis=0), "space", 1)
    half = keep + got[:rows]
    gathered = jnp.concatenate([coarse, got[rows:]], axis=0)
    for step in range(n_dp + n_space):
        if step < n_space:
            got = crossed(jnp.concatenate([half, gathered], axis=0), step)
            gathered = jnp.concatenate([gathered, got[rows:]], axis=0)
            got = got[:rows]
        else:
            got = crossed(half, step)
        half = half + got
    got = swapped(jnp.concatenate([half, gathered], axis=0), "space", 1)
    gathered = jnp.where(core == 1, gathered, got[rows:])
    return half, got[:rows], gathered


def picked(values, chosen):
    return jnp.einsum("jpb,jbq->pq", values, chosen.astype(jnp.float32), precision=lax.Precision.HIGHEST)


def on_device(
    fields,
    land_mask,
    land_frac,
    owner_map,
    targets,
    conv_weight,
    conv_bias,
    mix_weight,
    mix_bias,
    out_weight,
    out_bias,
):
    peers = lax.axis_size("space")
    position = lax.axis_index("space")
    pools = out_weight.shape[1]
    tile_rows = fields.shape[2]
    tile_cols = fields.shape[3]
    blocks = tile_rows // SIDE * (tile_cols // SIDE)
    serial = jnp.arange(peers, dtype=jnp.int32)
    local = jnp.arange(blocks, dtype=jnp.int32)
    extended = padded_2(fields, (("space", 2),), 1)
    target_rows = pools * blocks // 128
    target_all = gather_relative(targets.reshape(target_rows, 128), "space", bits_of(peers, 1))
    target_all = target_all.reshape(peers, pools, blocks)
    owners = lax.dynamic_slice_in_dim(owner_map, position * blocks, blocks)
    places = (position ^ serial)[:, None] * blocks + local[None, :]
    target_strip = picked(target_all, places[:, :, None] == owners[None, None, :])

    padded = jnp.pad(extended, ((0, 0), (0, 0), (0, 0), (1, 1)))
    outputs = forward_tile(
        padded, conv_weight, conv_bias, mix_weight, mix_bias, out_weight, out_bias
    )
    weight_map = land_frac * land_mask.astype(jnp.float32)
    density = jax.nn.softplus(outputs[5]) * weight_map
    strip_values = block_sums(density, SIDE)[0]
    denom = jnp.maximum(block_sums(weight_map, SIDE), 1.0)
    coarse = strip_values / denom
    residual = coarse - target_strip
    count_all = lax.axis_size("dp") * pools * owner_map.shape[0]
    d_block = (residual / (math.sqrt(count_all) * denom))[None]
    grads = backward_tile(*outputs, weight_map, d_block, mix_weight, out_weight, SIDE)
    width = mix_weight.shape[0]
    spare = jnp.zeros((16 - pools, width), jnp.float32)
    small = jnp.zeros((32, width), jnp.float32)
    small = small.at[0].set(grads[1]).at[1].set(grads[3]).at[2, :pools].set(grads[5])
    small = small.at[3].set(jnp.sum(residual * residual))
    payload = jnp.concatenate([grads[0], grads[2], small, grads[4].T, spare], axis=0)
    payload = jnp.pad(payload, ((0, -payload.shape[0] % 16), (0, 0)))
    half_rows = payload.shape[0] // 2
    core = position % 2
    low, high = payload[:half_rows], payload[half_rows:]
    half, other, gathered = reduce_all(
        jnp.where(core == 0, low, high),
        jnp.where(core == 0, high, low),
        coarse.reshape(target_rows, 128),
    )
    total = jnp.concatenate(
        [jnp.where(core == 0, half, other), jnp.where(core == 0, other, half)], axis=0
    )
    base = position | 1
    strips = owner_map.reshape(peers, blocks)[base ^ serial]
    coarse_pred = picked(
        gathered.reshape(peers, pools, blocks),
        strips[:, :, None] == (position * blocks + local)[None, None, :],
    )
    k = grads[0].shape[0]
    conv_grad = total[:k].reshape(conv_weight.shape)
    mix_grad = total[k : k + width]
    small = total[k + width : k + width + 32]
    out_grad = total[k + width + 32 : k + width + 32 + pools].T
    loss = 0.5 * small[3, 0] / count_all
    return (
        coarse_pred[None],
        conv_grad,
        small[0],
        mix_grad,
        small[1],
        out_grad,
        small[2, :pools],
        loss,
    )


def solution(mesh):
    placed = (
        P("dp", None, "space", None),
        P("space", None),
        P("space", None),
        P(),
        P("dp", None, "space"),
        P(),
        P(),
        P(),
        P(),
        P(),
        P(),
    )
    return jax.shard_map(
        on_device,
        mesh=mesh,
        in_specs=placed,
        out_specs=(P("dp", None, "space"), P(), P(), P(), P(), P(), P(), P()),
        check_vma=False,
    )
```

```python
import functools
import math

import jax
import jax.numpy as jnp
from jax import lax
from jax.experimental import pallas as pl
from jax.experimental.pallas import tpu as pltpu
from jax.sharding import PartitionSpec as P

SIDE = 8
POOL_ROWS = 16
GROUP = 2
VMEM = 56 * 1024 * 1024

CUBIC = 0.044715
ROOT_TWO_PI = math.sqrt(2.0 / math.pi)

F32, BF16 = jnp.float32, jnp.bfloat16


def gelu_pair(pre):
    square = pre * pre
    half = 0.5 + 0.5 * jnp.tanh(pre * (ROOT_TWO_PI + (ROOT_TWO_PI * CUBIC) * square))
    value = pre * half
    slope = half + value * (1.0 - half) * (2.0 * ROOT_TWO_PI + (6.0 * ROOT_TWO_PI * CUBIC) * square)
    return value, slope


def mm(left, right):
    return jnp.dot(left, right, preferred_element_type=F32)


def mm_nt(left, right):
    return lax.dot_general(left, right, (((1,), (1,)), ((), ())), preferred_element_type=F32)


def thirds(values):
    high = values.astype(BF16)
    rest = values - high.astype(F32)
    middle = rest.astype(BF16)
    low = (rest - middle.astype(F32)).astype(BF16)
    return jnp.concatenate([high, middle, low], axis=0)


def picked(values, chosen):
    rows = values.shape[0]
    out = mm(thirds(values), chosen)
    return out[:rows] + out[rows : 2 * rows] + out[2 * rows :]


def ones_where(condition):
    return jnp.where(condition, 1.0, 0.0).astype(BF16)


def iota(shape, dim):
    return lax.broadcasted_iota(jnp.int32, shape, dim)


def column(row, rows):
    return jnp.broadcast_to(row, (rows, row.shape[1])).T


def step_kernel(
    count_all,
    fields_ref,
    low_ref,
    high_ref,
    frac_ref,
    mask_ref,
    owner_ref,
    target_ref,
    w1_ref,
    b1_ref,
    w2_ref,
    b2_ref,
    w3_ref,
    b3_ref,
    keep_ref,
    send_ref,
    coarse_ref,
    shifted,
    weight,
    w1t,
    w2t,
    w3p,
    w3t,
    b1c,
    b2c,
    b3c,
    hidden_one,
    slope_one,
    hidden_two,
    slope_two,
    raw_all,
    sums,
    d_cols,
    total,
):
    rows, channels, cols = fields_ref.shape
    width = w2_ref.shape[0]
    pools = w3_ref.shape[1]
    peers, blocks = owner_ref.shape
    tiles = rows // SIDE
    across = cols // SIDE
    taps = 3 * channels
    lanes = GROUP * cols
    groups = SIDE // GROUP
    position = lax.axis_index("space")
    core = lax.rem(position, 2)

    w1t[...] = w1_ref[...].astype(F32).T.astype(BF16)
    w2t[...] = w2_ref[...].astype(F32).T.astype(BF16)
    w3f = jnp.concatenate(
        [w3_ref[...].astype(F32), jnp.zeros((width, width - pools), F32)], axis=1
    ).T[:POOL_ROWS]
    w3t[...] = w3f.astype(BF16)
    w3p[...] = jnp.concatenate([w3f, jnp.zeros((width - POOL_ROWS, width), F32)], axis=0).T[
        :, :POOL_ROWS
    ].astype(BF16)
    b1c[...] = column(b1_ref[...], width)
    b2c[...] = column(b2_ref[...], width)
    b3 = jnp.concatenate([b3_ref[...], jnp.zeros((1, width - pools), F32)], axis=1)
    b3c[...] = column(b3, width)[:POOL_ROWS]
    weight[...] = frac_ref[...] * mask_ref[...].astype(F32)

    lane = iota((channels, cols), 1)

    def put(row, values):
        values32 = values.astype(F32)
        left = jnp.where(lane == 0, 0.0, pltpu.roll(values32, 1, 1))
        right = jnp.where(lane == cols - 1, 0.0, pltpu.roll(values32, cols - 1, 1))
        shifted[pl.ds(pl.multiple_of(row * taps, taps), taps), :] = jnp.concatenate(
            [left.astype(BF16), values, right.astype(BF16)], axis=0
        )

    put(0, low_ref[...])
    put(rows + 1, high_ref[...])

    @pl.loop(0, rows // 8)
    def _(step):
        for inner in range(8):
            put(step * 8 + inner + 1, fields_ref[step * 8 + inner])

    def taps_of(row, count):
        parts = [
            shifted[pl.ds(pl.multiple_of((row + i) * taps, taps), 3 * taps), :]
            for i in range(count)
        ]
        return jnp.concatenate(parts, axis=1)

    def wide(values, count):
        return jnp.concatenate([values] * count, axis=1)

    def weights_of(row, count):
        parts = [
            jnp.broadcast_to(weight[pl.ds(row + i, 1), :], (POOL_ROWS, cols)) for i in range(count)
        ]
        return jnp.concatenate(parts, axis=1)

    @pl.loop(0, tiles)
    def _(tile):
        total_cols = jnp.zeros((POOL_ROWS, cols), F32)
        for group in range(groups):
            row = tile * SIDE + group * GROUP
            at = tile * groups + group
            pre_one = mm(w1t[...], taps_of(row, GROUP)) + wide(b1c[...], GROUP)
            value_one, slope = gelu_pair(pre_one)
            slope_one[at] = slope
            value_one = value_one.astype(BF16)
            hidden_one[at] = value_one
            pre_two = mm(w2t[...], value_one) + wide(b2c[...], GROUP)
            value_two, slope = gelu_pair(pre_two)
            slope_two[at] = slope
            value_two = value_two.astype(BF16)
            hidden_two[at] = value_two
            raw = mm(w3t[...], value_two) + wide(b3c[...], GROUP)
            raw_all[at] = raw
            density = (
                jnp.maximum(raw, 0.0) + jnp.log1p(jnp.exp(-jnp.abs(raw)))
            ) * weights_of(row, GROUP)
            for i in range(GROUP):
                total_cols = total_cols + density[:, i * cols : (i + 1) * cols]
        sums[pl.ds(pl.multiple_of(tile * POOL_ROWS, POOL_ROWS), POOL_ROWS), :] = total_cols

    weight_cols = jnp.sum(weight[...].reshape(tiles, SIDE, cols), axis=1)
    weight_cols = jnp.concatenate([weight_cols, jnp.zeros((-tiles % 8, cols), F32)], axis=0)
    same = ones_where(iota((cols, cols), 0) // SIDE == iota((cols, cols), 1) // SIDE)
    summed = picked(jnp.concatenate([sums[...], weight_cols], axis=0), same)
    owners = owner_ref[pl.ds(position, 1), :]
    target = jnp.zeros((POOL_ROWS, blocks), F32)
    for peer in range(peers):
        places = iota((blocks, blocks), 0) + (position ^ peer) * blocks
        values = jnp.concatenate(
            [target_ref[peer], jnp.zeros((POOL_ROWS - pools, blocks), F32)], axis=0
        )
        target = target + picked(values, ones_where(places == owners))
    in_tile = iota((blocks, cols), 0) - iota((blocks, cols), 1) // SIDE
    spread = jnp.concatenate([ones_where(in_tile == tile * across) for tile in range(tiles)], axis=1)
    target_cols = picked(target, spread)
    first = iota((cols, blocks), 0)
    in_block = iota((cols, blocks), 1) - first // SIDE
    coarse = jnp.zeros((POOL_ROWS, blocks), F32)
    loss = jnp.zeros((POOL_ROWS, cols), F32)
    valid = iota((POOL_ROWS, cols), 0) < pools
    for tile in range(tiles):
        denom = jnp.maximum(summed[tiles * POOL_ROWS + tile : tiles * POOL_ROWS + tile + 1], 1.0)
        pred = summed[tile * POOL_ROWS : (tile + 1) * POOL_ROWS] / denom
        residual = jnp.where(valid, pred - target_cols[:, tile * cols : (tile + 1) * cols], 0.0)
        loss = loss + residual * residual
        d_cols[tile] = residual / (math.sqrt(count_all) * denom)
        leads = (first % SIDE == 0) & (in_block == tile * across)
        coarse = coarse + picked(pred, ones_where(leads))
    loss = jnp.sum(jnp.sum(loss, axis=1, keepdims=True), axis=0, keepdims=True) * (1.0 / SIDE)
    coarse_rows = jnp.concatenate(
        [
            coarse[:, :128],
            jnp.concatenate([coarse[:, 128:], jnp.zeros((POOL_ROWS, 256 - blocks), F32)], axis=1),
        ],
        axis=0,
    )
    coarse_ref[...] = coarse_rows

    total[...] = jnp.zeros_like(total)
    ones = jnp.ones((POOL_ROWS, SIDE * cols), BF16)
    conv_rows = 3 * taps
    mix_at = conv_rows
    out_at = mix_at + width
    bias_at = out_at + POOL_ROWS

    @pl.loop(0, tiles, init_carry=jnp.zeros((POOL_ROWS, cols), F32))
    def out_bias(tile, carried):
        d_raws, d_twos, d_ones = [], [], []
        for group in range(groups):
            row = tile * SIDE + group * GROUP
            at = tile * groups + group
            raw = raw_all[at]
            small = jnp.exp(-jnp.abs(raw))
            sigmoid = jnp.where(raw >= 0.0, 1.0, small) / (1.0 + small)
            d_raw = (wide(d_cols[tile], GROUP) * weights_of(row, GROUP) * sigmoid).astype(BF16)
            d_two = (mm(w3p[...], d_raw) * slope_two[at]).astype(BF16)
            d_one = (mm(w2_ref[...], d_two) * slope_one[at]).astype(BF16)
            for i in range(GROUP):
                carried = carried + d_raw[:, i * cols : (i + 1) * cols].astype(F32)
            d_raws.append(d_raw)
            d_twos.append(d_two)
            d_ones.append(d_one)
        at = tile * groups
        d_raw = jnp.concatenate(d_raws, axis=1)
        d_two = jnp.concatenate(d_twos, axis=1)
        d_one = jnp.concatenate(d_ones, axis=1)
        inputs = jnp.concatenate([taps_of(tile * SIDE, SIDE), ones], axis=0)
        got = mm_nt(inputs, d_one)
        total[:conv_rows, :] += got[:conv_rows]
        total[bias_at : bias_at + 8, :] += got[conv_rows : conv_rows + 8]
        one = jnp.concatenate([hidden_one[at + g] for g in range(groups)], axis=1)
        got = mm_nt(jnp.concatenate([one, ones], axis=0), d_two)
        total[mix_at:out_at, :] += got[:width]
        total[bias_at + 8 : bias_at + 16, :] += got[width : width + 8]
        two = jnp.concatenate([hidden_two[at + g] for g in range(groups)], axis=1)
        total[out_at:bias_at, :] += mm_nt(d_raw, two)
        return carried

    bias = jnp.sum(out_bias, axis=1, keepdims=True)
    here, there = iota((POOL_ROWS, cols), 0), iota((POOL_ROWS, cols), 1)
    bias_row = jnp.sum(jnp.where(here == there, bias, 0.0), axis=0, keepdims=True)
    part = total[out_at:bias_at, :]
    part = jnp.where(here == pools, bias_row, part)
    total[out_at:bias_at, :] = jnp.where(here == pools + 1, loss, part)
    half = keep_ref.shape[0]
    keep_ref[...] = total[pl.ds(pl.multiple_of(core * half, 8), half), :]
    send_ref[:half, :] = total[pl.ds(pl.multiple_of((1 - core) * half, 8), half), :]
    send_ref[half:, :] = coarse_rows


def finish_kernel(
    count_all,
    half_ref,
    other_ref,
    gathered_ref,
    owner_ref,
    coarse_ref,
    conv_ref,
    conv_bias_ref,
    mix_ref,
    mix_bias_ref,
    out_ref,
    out_bias_ref,
    loss_ref,
):
    position = lax.axis_index("space")
    core = lax.rem(position, 2)
    peers, blocks = owner_ref.shape
    pools = out_ref.shape[0]
    conv_rows, width = conv_ref.shape
    half, other = half_ref[...], other_ref[...]
    low = jnp.where(core == 0, half, other)
    high = jnp.where(core == 0, other, half)
    total = jnp.concatenate([low, high], axis=0)
    out_at = conv_rows + width
    bias_at = out_at + POOL_ROWS
    conv_ref[...] = total[:conv_rows]
    mix_ref[...] = total[conv_rows:out_at]
    out_ref[...] = total[out_at : out_at + pools]
    out_bias_ref[...] = total[out_at + pools : out_at + pools + 1, :pools]
    loss_ref[...] = (0.5 / count_all) * total[out_at + pools + 1 : out_at + pools + 2, :1]
    conv_bias_ref[...] = total[bias_at : bias_at + 1]
    mix_bias_ref[...] = total[bias_at + 8 : bias_at + 9]
    base = position | 1
    coarse = jnp.zeros((POOL_ROWS, blocks), F32)
    for peer in range(peers):
        owners = owner_ref[pl.ds(base ^ peer, 1), :]
        places = iota((blocks, blocks), 0) + position * blocks
        values = jnp.concatenate(
            [
                gathered_ref[peer, :POOL_ROWS, :],
                gathered_ref[peer, POOL_ROWS:, : blocks - 128],
            ],
            axis=1,
        )
        terms = thirds(values)
        got = mm_nt(terms, ones_where(places == owners))
        coarse = coarse + got[:POOL_ROWS] + got[POOL_ROWS : 2 * POOL_ROWS] + got[2 * POOL_ROWS :]
    coarse_ref[...] = coarse[:pools]


def bits_of(size, low):
    return [1 << k for k in range(size.bit_length() - 1) if (1 << k) >= low]


def swapped(values, axis, bit):
    return lax.ppermute(values, axis, [(i, i ^ bit) for i in range(lax.axis_size(axis))])


def gather_relative(values, axis, bits):
    for bit in bits:
        values = jnp.concatenate([values, swapped(values, axis, bit)], axis=0)
    return values


def crossed(values, step):
    dp, space = lax.axis_size("dp"), lax.axis_size("space")
    dp_moves = [(bit, 0) for bit in bits_of(dp, 1)]
    space_moves = [(0, bit) for bit in bits_of(space, 2)]
    orders = (dp_moves + space_moves, space_moves + dp_moves)
    pairs = []
    for d in range(dp):
        for s in range(space):
            d_bit, s_bit = orders[s % 2][step]
            pairs.append((d * space + s, (d ^ d_bit) * space + (s ^ s_bit)))
    return lax.ppermute(values, ("dp", "space"), pairs)


def reduce_all(keep, send, coarse):
    space = lax.axis_size("space")
    n_dp, n_space = len(bits_of(lax.axis_size("dp"), 1)), len(bits_of(space, 2))
    core = lax.axis_index("space") % 2
    rows = keep.shape[0]
    got = swapped(send, "space", 1)
    half = keep + got[:rows]
    gathered = jnp.concatenate([coarse, got[rows:]], axis=0)
    for step in range(n_dp + n_space):
        if step < n_space:
            got = crossed(jnp.concatenate([half, gathered], axis=0), step)
            gathered = jnp.concatenate([gathered, got[rows:]], axis=0)
            got = got[:rows]
        else:
            got = crossed(half, step)
        half = half + got
    got = swapped(jnp.concatenate([half, gathered], axis=0), "space", 1)
    gathered = jnp.where(core == 1, gathered, got[rows:])
    return half, got[:rows], gathered


def on_device(
    fields,
    land_mask,
    land_frac,
    owner_map,
    targets,
    conv_weight,
    conv_bias,
    mix_weight,
    mix_bias,
    out_weight,
    out_bias,
):
    peers = lax.axis_size("space")
    pools = out_weight.shape[1]
    width = mix_weight.shape[0]
    channels, rows, cols = fields.shape[1:]
    tiles = rows // SIDE
    blocks = tiles * (cols // SIDE)
    count_all = lax.axis_size("dp") * pools * owner_map.shape[0]
    owners = owner_map.reshape(peers, blocks)

    by_row = jnp.swapaxes(fields[0], 0, 1)
    forward = [(i, i + 1) for i in range(peers - 1)]
    backward = [(target, source) for source, target in forward]
    low = lax.ppermute(by_row[rows - 1], "space", forward)
    high = lax.ppermute(by_row[0], "space", backward)
    target_all = gather_relative(targets, "space", bits_of(peers, 1))

    conv_rows = 9 * channels
    half = conv_rows + width + 2 * POOL_ROWS
    half = (half + 31) // 32 * 16
    groups = rows // GROUP
    lanes = GROUP * cols
    f32, bf16 = F32, BF16
    keep, send, coarse = pl.pallas_call(
        functools.partial(step_kernel, count_all),
        out_shape=[
            jax.ShapeDtypeStruct((half, width), f32),
            jax.ShapeDtypeStruct((half + 2 * POOL_ROWS, width), f32),
            jax.ShapeDtypeStruct((2 * POOL_ROWS, width), f32),
        ],
        in_specs=[pl.BlockSpec(memory_space=pltpu.VMEM)] * 13,
        out_specs=[pl.BlockSpec(memory_space=pltpu.VMEM)] * 3,
        scratch_shapes=[
            pltpu.VMEM(((rows + 2) * 3 * channels, cols), bf16),
            pltpu.VMEM((rows, cols), f32),
            pltpu.VMEM((width, conv_rows), bf16),
            pltpu.VMEM((width, width), bf16),
            pltpu.VMEM((width, POOL_ROWS), bf16),
            pltpu.VMEM((POOL_ROWS, width), bf16),
            pltpu.VMEM((width, cols), f32),
            pltpu.VMEM((width, cols), f32),
            pltpu.VMEM((POOL_ROWS, cols), f32),
            pltpu.VMEM((groups, width, lanes), bf16),
            pltpu.VMEM((groups, width, lanes), f32),
            pltpu.VMEM((groups, width, lanes), bf16),
            pltpu.VMEM((groups, width, lanes), f32),
            pltpu.VMEM((groups, POOL_ROWS, lanes), f32),
            pltpu.VMEM((tiles * POOL_ROWS, cols), f32),
            pltpu.VMEM((tiles, POOL_ROWS, cols), f32),
            pltpu.VMEM((2 * half, width), f32),
        ],
        compiler_params=pltpu.CompilerParams(vmem_limit_bytes=VMEM),
        name="train_step",
    )(
        by_row,
        low,
        high,
        land_frac,
        land_mask,
        owners,
        target_all,
        conv_weight.reshape(conv_rows, width),
        conv_bias.reshape(1, width),
        mix_weight,
        mix_bias.reshape(1, width),
        out_weight,
        out_bias.reshape(1, pools),
    )
    half, other, gathered = reduce_all(keep, send, coarse)
    outs = pl.pallas_call(
        functools.partial(finish_kernel, count_all),
        out_shape=[
            jax.ShapeDtypeStruct((pools, blocks), f32),
            jax.ShapeDtypeStruct((conv_rows, width), f32),
            jax.ShapeDtypeStruct((1, width), f32),
            jax.ShapeDtypeStruct((width, width), f32),
            jax.ShapeDtypeStruct((1, width), f32),
            jax.ShapeDtypeStruct((pools, width), f32),
            jax.ShapeDtypeStruct((1, pools), f32),
            jax.ShapeDtypeStruct((1, 1), f32),
        ],
        in_specs=[pl.BlockSpec(memory_space=pltpu.VMEM)] * 4,
        out_specs=[pl.BlockSpec(memory_space=pltpu.VMEM)] * 8,
        compiler_params=pltpu.CompilerParams(vmem_limit_bytes=VMEM),
        name="finish",
    )(half, other, gathered.reshape(peers, 2 * POOL_ROWS, width), owners)
    coarse_pred, conv_grad, conv_bias_grad, mix_grad, mix_bias_grad, out_grad, out_bias_grad, loss = outs
    return (
        coarse_pred[None],
        conv_grad.reshape(conv_weight.shape),
        conv_bias_grad.reshape(width),
        mix_grad,
        mix_bias_grad.reshape(width),
        out_grad.T,
        out_bias_grad.reshape(pools),
        loss.reshape(()),
    )


def solution(mesh):
    placed = (
        P("dp", None, "space", None),
        P("space", None),
        P("space", None),
        P(),
        P("dp", None, "space"),
        P(),
        P(),
        P(),
        P(),
        P(),
        P(),
    )
    return jax.shard_map(
        on_device,
        mesh=mesh,
        in_specs=placed,
        out_specs=(P("dp", None, "space"), P(), P(), P(), P(), P(), P(), P()),
        check_vma=False,
    )
```

```python
import functools
import math

import jax
import jax.numpy as jnp
from jax import lax
from jax.experimental import pallas as pl
from jax.experimental.pallas import tpu as pltpu
from jax.sharding import PartitionSpec as P

SIDE = 8
POOL_ROWS = 16
GROUP = 2
VMEM = 40 * 1024 * 1024

CUBIC = 0.044715
ROOT_TWO_PI = math.sqrt(2.0 / math.pi)

F32, BF16 = jnp.float32, jnp.bfloat16


def gelu_pair(pre):
    square = pre * pre
    half = 0.5 + 0.5 * jnp.tanh(pre * (ROOT_TWO_PI + (ROOT_TWO_PI * CUBIC) * square))
    value = pre * half
    slope = half + value * (1.0 - half) * (2.0 * ROOT_TWO_PI + (6.0 * ROOT_TWO_PI * CUBIC) * square)
    return value, slope


def mm(left, right):
    return jnp.dot(left, right, preferred_element_type=F32)


def mm_nt(left, right):
    return lax.dot_general(left, right, (((1,), (1,)), ((), ())), preferred_element_type=F32)


def thirds(values):
    high = values.astype(BF16)
    rest = values - high.astype(F32)
    middle = rest.astype(BF16)
    low = (rest - middle.astype(F32)).astype(BF16)
    return jnp.concatenate([high, middle, low], axis=0)


def picked(values, chosen):
    rows = values.shape[0]
    out = mm(thirds(values), chosen)
    return out[:rows] + out[rows : 2 * rows] + out[2 * rows :]


def ones_where(condition):
    return jnp.where(condition, 1.0, 0.0).astype(BF16)


def iota(shape, dim):
    return lax.broadcasted_iota(jnp.int32, shape, dim)


def owners_of(owner_ref, strip, blocks):
    at = strip * blocks
    row = at // 128
    pair = jnp.concatenate([owner_ref[pl.ds(row, 1), :], owner_ref[pl.ds(row + 1, 1), :]], axis=1)
    return jnp.where(at % 128 == 0, pair, pltpu.roll(pair, 256 - blocks % 128, 1))[:, :blocks]


def step_kernel(
    count_all,
    fields_ref,
    paired_ref,
    chained_ref,
    frac_ref,
    mask_ref,
    owner_ref,
    target_ref,
    w1_ref,
    b1_ref,
    w2_ref,
    b2_ref,
    w3t_ref,
    b3_ref,
    keep_ref,
    send_ref,
    coarse_ref,
    shifted,
    weight,
    w1t,
    w2t,
    w3t,
    w3p,
    pre_one,
    hidden_one,
    slope_one,
    hidden_two,
    slope_two,
    raw_all,
    scale,
    d_raw_all,
    d_two_all,
    d_one_all,
    total,
):
    rows, channels, cols = fields_ref.shape
    width = w2_ref.shape[0]
    pools = w3t_ref.shape[0]
    blocks = target_ref.shape[2]
    peers = target_ref.shape[0] // pools
    tiles = rows // SIDE
    across = cols // SIDE
    taps = 3 * channels
    conv_rows = 3 * taps
    cells = SIDE * cols
    position = lax.axis_index("space")
    core = lax.rem(position, 2)

    def with_bias(weights, bias):
        high = bias.astype(BF16).astype(F32)
        middle = (bias - high).astype(BF16).astype(F32)
        low = bias - high - middle
        fill = jnp.zeros((POOL_ROWS - 3, bias.shape[1]), F32)
        return jnp.concatenate([weights, high, middle, low, fill], axis=0).T

    w1t[...] = with_bias(w1_ref[...].astype(F32), b1_ref[...]).astype(BF16)
    w2t[...] = with_bias(w2_ref[...].astype(F32), b2_ref[...]).astype(BF16)
    w3f = jnp.concatenate([w3t_ref[...].astype(F32), jnp.zeros((width - pools, width), F32)], axis=0).T
    w3p[...] = w3f[:, :POOL_ROWS].astype(BF16)
    b3 = jnp.concatenate([b3_ref[...], jnp.zeros((1, width - pools), F32)], axis=1)
    w3t[...] = with_bias(w3f, b3)[:POOL_ROWS].astype(BF16)
    weight[...] = frac_ref[...] * mask_ref[...].astype(F32)

    lane = iota((channels, cols), 1)

    def put(row, values):
        values32 = values.astype(F32)
        left = jnp.where(lane == 0, 0.0, pltpu.roll(values32, 1, 1))
        right = jnp.where(lane == cols - 1, 0.0, pltpu.roll(values32, cols - 1, 1))
        shifted[pl.ds(pl.multiple_of(row * taps, taps), taps), :] = jnp.concatenate(
            [left.astype(BF16), values, right.astype(BF16)], axis=0
        )

    paired, chained = paired_ref[...].astype(F32), chained_ref[...].astype(F32)
    put(0, jnp.where(core == 0, chained, paired).astype(BF16))
    put(rows + 1, jnp.where(core == 0, paired, chained).astype(BF16))

    @pl.loop(0, rows // 8)
    def _(step):
        for inner in range(8):
            put(step * 8 + inner + 1, fields_ref[step * 8 + inner])

    ones = jnp.ones((POOL_ROWS, cells), BF16)

    def taps_of(row, count):
        parts = [
            shifted[pl.ds(pl.multiple_of((row + i) * taps, taps), conv_rows), :]
            for i in range(count)
        ]
        return jnp.concatenate(
            [jnp.concatenate(parts, axis=1), ones[:, : count * cols]], axis=0
        )

    def wide(values, count):
        return jnp.concatenate([values] * count, axis=1)

    part = GROUP * cols
    parts = [slice(at, at + part) for at in range(0, cells, part)]

    def first_layer(tile):
        for group, here in enumerate(parts):
            pre_one[lax.rem(tile, 2), :, here] = mm(w1t[...], taps_of(tile * SIDE + group * GROUP, GROUP))

    hidden_two[0] = jnp.zeros(hidden_two.shape[1:], BF16)
    first_layer(0)

    @pl.loop(0, tiles)
    def _(tile):
        following = jnp.minimum(tile + 1, tiles - 1)
        now = lax.rem(tile, 2)
        pre_twos = []
        for group, here in enumerate(parts):
            ahead = mm(w1t[...], taps_of(following * SIDE + group * GROUP, GROUP))
            value, slope = gelu_pair(pre_one[now, :, here])
            value = value.astype(BF16)
            hidden_one[tile, :, here] = value
            slope_one[tile, :, here] = slope
            pre_one[1 - now, :, here] = ahead
            pre_twos.append(mm(w2t[...], jnp.concatenate([value, ones[:, :part]], axis=0)))
        raw_all[tile] = mm(w3t[...], jnp.concatenate([hidden_two[tile], ones], axis=0))
        for here, pre_two in zip(parts, pre_twos):
            value, slope = gelu_pair(pre_two)
            hidden_two[tile + 1, :, here] = value.astype(BF16)
            slope_two[tile, :, here] = slope

    raw_all[tiles] = mm(w3t[...], jnp.concatenate([hidden_two[tiles], ones], axis=0))

    sums = []
    for tile in range(tiles):
        raw = raw_all[tile + 1]
        weights = jnp.concatenate(
            [
                jnp.broadcast_to(weight[tile * SIDE + i : tile * SIDE + i + 1, :], (POOL_ROWS, cols))
                for i in range(SIDE)
            ],
            axis=1,
        )
        small = jnp.exp(-jnp.abs(raw))
        density = (jnp.maximum(raw, 0.0) + jnp.log1p(small)) * weights
        scale[tile] = jnp.where(raw >= 0.0, 1.0, small) / (1.0 + small) * weights
        sums.append(sum(density[:, i * cols : (i + 1) * cols] for i in range(SIDE)))
    weight_cols = jnp.sum(weight[...].reshape(tiles, SIDE, cols), axis=1)
    weight_cols = jnp.concatenate([weight_cols, jnp.zeros((-tiles % 8, cols), F32)], axis=0)
    same = ones_where(iota((cols, cols), 0) // SIDE == iota((cols, cols), 1) // SIDE)
    summed = picked(jnp.concatenate(sums + [weight_cols], axis=0), same)
    owners = owners_of(owner_ref, position, blocks)
    target = jnp.zeros((POOL_ROWS, blocks), F32)
    for peer in range(peers):
        places = iota((blocks, blocks), 0) + (position ^ peer) * blocks
        values = jnp.concatenate(
            [
                target_ref[peer * pools : (peer + 1) * pools, 0, :],
                jnp.zeros((POOL_ROWS - pools, blocks), F32),
            ],
            axis=0,
        )
        target = target + picked(values, ones_where(places == owners))
    in_tile = iota((blocks, cols), 0) - iota((blocks, cols), 1) // SIDE
    spread = jnp.concatenate([ones_where(in_tile == tile * across) for tile in range(tiles)], axis=1)
    target_cols = picked(target, spread)
    first = iota((cols, blocks), 0)
    in_block = iota((cols, blocks), 1) - first // SIDE
    coarse = jnp.zeros((POOL_ROWS, blocks), F32)
    loss = jnp.zeros((POOL_ROWS, cols), F32)
    valid = iota((POOL_ROWS, cols), 0) < pools
    out_bias = jnp.zeros((POOL_ROWS, cols), F32)
    for tile in range(tiles):
        denom = jnp.maximum(summed[tiles * POOL_ROWS + tile : tiles * POOL_ROWS + tile + 1], 1.0)
        pred = summed[tile * POOL_ROWS : (tile + 1) * POOL_ROWS] / denom
        residual = jnp.where(valid, pred - target_cols[:, tile * cols : (tile + 1) * cols], 0.0)
        loss = loss + residual * residual
        d_cols = residual / (math.sqrt(count_all) * denom)
        d_raw = (wide(d_cols, SIDE) * scale[tile]).astype(BF16)
        d_raw_all[tile] = d_raw
        d_raw = d_raw.astype(F32)
        out_bias = out_bias + sum(d_raw[:, i * cols : (i + 1) * cols] for i in range(SIDE))
        leads = (first % SIDE == 0) & (in_block == tile * across)
        coarse = coarse + picked(pred, ones_where(leads))
    loss = jnp.sum(jnp.sum(loss, axis=1, keepdims=True), axis=0, keepdims=True) * (1.0 / SIDE)
    coarse_rows = jnp.concatenate(
        [
            coarse[:, :128],
            jnp.concatenate([coarse[:, 128:], jnp.zeros((POOL_ROWS, 256 - blocks), F32)], axis=1),
        ],
        axis=0,
    )
    coarse_ref[...] = coarse_rows

    mix_at = conv_rows
    out_at = mix_at + width
    bias_at = out_at + POOL_ROWS
    total[...] = jnp.zeros_like(total)

    def through(tile):
        now = lax.rem(tile, 2)
        d_twos = []
        for here in parts:
            d_two = (mm(w3p[...], d_raw_all[tile, :, here]) * slope_two[tile, :, here]).astype(BF16)
            d_two_all[now, :, here] = d_two
            d_twos.append(d_two)
        for here, d_two in zip(parts, d_twos):
            d_one = mm(w2_ref[...], d_two) * slope_one[tile, :, here]
            d_one_all[now, :, here] = d_one.astype(BF16)

    def add_up(tile):
        now = lax.rem(tile, 2)
        total[out_at:bias_at, :] += mm_nt(d_raw_all[tile], hidden_two[tile + 1])
        got = mm_nt(jnp.concatenate([hidden_one[tile], ones], axis=0), d_two_all[now])
        total[mix_at:out_at, :] += got[:width]
        total[bias_at + 8 : bias_at + 16, :] += got[width : width + 8]
        got = mm_nt(taps_of(tile * SIDE, SIDE), d_one_all[now])
        total[:conv_rows, :] += got[:conv_rows]
        total[bias_at : bias_at + 8, :] += got[conv_rows : conv_rows + 8]

    through(0)

    @pl.loop(1, tiles)
    def _(tile):
        add_up(tile - 1)
        through(tile)

    add_up(tiles - 1)

    bias = jnp.sum(out_bias, axis=1, keepdims=True)
    here, there = iota((POOL_ROWS, cols), 0), iota((POOL_ROWS, cols), 1)
    bias_row = jnp.sum(jnp.where(here == there, bias, 0.0), axis=0, keepdims=True)
    last = total[out_at:bias_at, :]
    last = jnp.where(here == pools, bias_row, last)
    total[out_at:bias_at, :] = jnp.where(here == pools + 1, loss, last)
    half = keep_ref.shape[0]
    keep_ref[...] = total[pl.ds(pl.multiple_of(core * half, 8), half), :]
    send_ref[:half, :] = total[pl.ds(pl.multiple_of((1 - core) * half, 8), half), :]
    send_ref[half:, :] = coarse_rows


def finish_kernel(
    count_all,
    mine_ref,
    other_ref,
    owner_ref,
    coarse_ref,
    conv_ref,
    conv_bias_ref,
    mix_ref,
    mix_bias_ref,
    out_ref,
    out_bias_ref,
    loss_ref,
):
    position = lax.axis_index("space")
    core = lax.rem(position, 2)
    pools, _, blocks = coarse_ref.shape
    conv_rows, width = conv_ref.shape
    out_at = conv_rows + width
    bias_at = out_at + POOL_ROWS
    half = (bias_at + POOL_ROWS) // 2
    peers = (mine_ref.shape[0] - half) // (2 * POOL_ROWS)
    mine, other = mine_ref[...], other_ref[...]
    low = jnp.where(core == 0, mine[:half], other[:half])
    high = jnp.where(core == 0, other[:half], mine[:half])
    gathered = jnp.where(core == 1, mine[half:], other[half:])
    total = jnp.concatenate([low, high], axis=0)
    conv_ref[...] = total[:conv_rows]
    mix_ref[...] = total[conv_rows:out_at]
    out_ref[...] = total[out_at : out_at + pools]
    out_bias_ref[...] = total[out_at + pools : out_at + pools + 1, :pools]
    loss_ref[...] = (0.5 / count_all) * total[out_at + pools + 1 : out_at + pools + 2, :1]
    conv_bias_ref[...] = total[bias_at : bias_at + 1]
    mix_bias_ref[...] = total[bias_at + 8 : bias_at + 9]
    base = position | 1
    coarse = jnp.zeros((POOL_ROWS, blocks), F32)
    for peer in range(peers):
        owners = owners_of(owner_ref, base ^ peer, blocks)
        places = iota((blocks, blocks), 0) + position * blocks
        at = peer * 2 * POOL_ROWS
        values = jnp.concatenate(
            [
                gathered[at : at + POOL_ROWS],
                gathered[at + POOL_ROWS : at + 2 * POOL_ROWS, : blocks - 128],
            ],
            axis=1,
        )
        got = mm_nt(thirds(values), ones_where(places == owners))
        coarse = coarse + got[:POOL_ROWS] + got[POOL_ROWS : 2 * POOL_ROWS] + got[2 * POOL_ROWS :]
    coarse_ref[:, 0, :] = coarse[:pools]


def bits_of(size, low):
    return [1 << k for k in range(size.bit_length() - 1) if (1 << k) >= low]


def swapped(values, axis, bit):
    return lax.ppermute(values, axis, [(i, i ^ bit) for i in range(lax.axis_size(axis))])


def gather_relative(values, axis, bits):
    for bit in bits:
        values = jnp.concatenate([values, swapped(values, axis, bit)], axis=0)
    return values


def crossed(values, step):
    dp, space = lax.axis_size("dp"), lax.axis_size("space")
    dp_moves = [(bit, 0) for bit in bits_of(dp, 1)]
    space_moves = [(0, bit) for bit in bits_of(space, 2)]
    orders = (dp_moves + space_moves, space_moves + dp_moves)
    pairs = []
    for d in range(dp):
        for s in range(space):
            d_bit, s_bit = orders[s % 2][step]
            pairs.append((d * space + s, (d ^ d_bit) * space + (s ^ s_bit)))
    return lax.ppermute(values, ("dp", "space"), pairs)


def reduce_all(keep, send, coarse):
    space = lax.axis_size("space")
    n_dp, n_space = len(bits_of(lax.axis_size("dp"), 1)), len(bits_of(space, 2))
    rows = keep.shape[0]
    got = swapped(send, "space", 1)
    half = keep + got[:rows]
    gathered = jnp.concatenate([coarse, got[rows:]], axis=0)
    for step in range(n_dp + n_space):
        if step < n_space:
            got = crossed(jnp.concatenate([half, gathered], axis=0), step)
            gathered = jnp.concatenate([gathered, got[rows:]], axis=0)
            got = got[:rows]
        else:
            got = crossed(half, step)
        half = half + got
    mine = jnp.concatenate([half, gathered], axis=0)
    return mine, swapped(mine, "space", 1)


def on_device(
    fields,
    land_mask,
    land_frac,
    owner_map,
    targets,
    conv_weight,
    conv_bias,
    mix_weight,
    mix_bias,
    out_weight,
    out_bias,
):
    peers = lax.axis_size("space")
    pools = out_weight.shape[1]
    width = mix_weight.shape[0]
    channels, rows, cols = fields.shape[1:]
    tiles = rows // SIDE
    blocks = tiles * (cols // SIDE)
    count_all = lax.axis_size("dp") * pools * owner_map.shape[0]
    owners = owner_map.reshape(-1, 128)
    core = lax.axis_index("space") % 2

    by_row = jnp.swapaxes(fields[0], 0, 1)
    top, bottom = by_row[0], by_row[rows - 1]
    chain = [(i, i + 1) for i in range(1, peers - 1, 2)]
    chain = chain + [(target, source) for source, target in chain]
    paired = swapped(jnp.where(core == 0, bottom, top), "space", 1)
    chained = lax.ppermute(jnp.where(core == 0, top, bottom), "space", chain)
    target_all = gather_relative(jnp.swapaxes(targets, 0, 1), "space", bits_of(peers, 1))

    conv_rows = 9 * channels
    half = conv_rows + width + 2 * POOL_ROWS
    half = (half + 31) // 32 * 16
    cells = SIDE * cols
    f32, bf16 = F32, BF16
    keep, send, coarse = pl.pallas_call(
        functools.partial(step_kernel, count_all),
        out_shape=[
            jax.ShapeDtypeStruct((half, width), f32),
            jax.ShapeDtypeStruct((half + 2 * POOL_ROWS, width), f32),
            jax.ShapeDtypeStruct((2 * POOL_ROWS, width), f32),
        ],
        in_specs=[pl.BlockSpec(memory_space=pltpu.VMEM)] * 13,
        out_specs=[pl.BlockSpec(memory_space=pltpu.VMEM)] * 3,
        scratch_shapes=[
            pltpu.VMEM(((rows + 2) * 3 * channels, cols), bf16),
            pltpu.VMEM((rows, cols), f32),
            pltpu.VMEM((width, conv_rows + POOL_ROWS), bf16),
            pltpu.VMEM((width, width + POOL_ROWS), bf16),
            pltpu.VMEM((POOL_ROWS, width + POOL_ROWS), bf16),
            pltpu.VMEM((width, POOL_ROWS), bf16),
            pltpu.VMEM((2, width, cells), f32),
            pltpu.VMEM((tiles, width, cells), bf16),
            pltpu.VMEM((tiles, width, cells), f32),
            pltpu.VMEM((tiles + 1, width, cells), bf16),
            pltpu.VMEM((tiles, width, cells), f32),
            pltpu.VMEM((tiles + 1, POOL_ROWS, cells), f32),
            pltpu.VMEM((tiles, POOL_ROWS, cells), f32),
            pltpu.VMEM((tiles, POOL_ROWS, cells), bf16),
            pltpu.VMEM((2, width, cells), bf16),
            pltpu.VMEM((2, width, cells), bf16),
            pltpu.VMEM((2 * half, width), f32),
        ],
        compiler_params=pltpu.CompilerParams(vmem_limit_bytes=VMEM),
        name="train_step",
    )(
        by_row,
        paired,
        chained,
        land_frac,
        land_mask,
        owners,
        target_all,
        conv_weight.reshape(conv_rows, width),
        conv_bias.reshape(1, width),
        mix_weight,
        mix_bias.reshape(1, width),
        out_weight.T,
        out_bias.reshape(1, pools),
    )
    mine, other = reduce_all(keep, send, coarse)
    outs = pl.pallas_call(
        functools.partial(finish_kernel, count_all),
        out_shape=[
            jax.ShapeDtypeStruct((pools, 1, blocks), f32),
            jax.ShapeDtypeStruct((conv_rows, width), f32),
            jax.ShapeDtypeStruct((1, width), f32),
            jax.ShapeDtypeStruct((width, width), f32),
            jax.ShapeDtypeStruct((1, width), f32),
            jax.ShapeDtypeStruct((pools, width), f32),
            jax.ShapeDtypeStruct((1, pools), f32),
            jax.ShapeDtypeStruct((1, 1), f32),
        ],
        in_specs=[pl.BlockSpec(memory_space=pltpu.VMEM)] * 3,
        out_specs=[pl.BlockSpec(memory_space=pltpu.VMEM)] * 8,
        compiler_params=pltpu.CompilerParams(vmem_limit_bytes=VMEM),
        name="finish",
    )(mine, other, owners)
    coarse_pred, conv_grad, conv_bias_grad, mix_grad, mix_bias_grad, out_grad, out_bias_grad, loss = outs
    return (
        jnp.swapaxes(coarse_pred, 0, 1),
        conv_grad.reshape(conv_weight.shape),
        conv_bias_grad.reshape(width),
        mix_grad,
        mix_bias_grad.reshape(width),
        out_grad.T,
        out_bias_grad.reshape(pools),
        loss.reshape(()),
    )


def solution(mesh):
    placed = (
        P("dp", None, "space", None),
        P("space", None),
        P("space", None),
        P(),
        P("dp", None, "space"),
        P(),
        P(),
        P(),
        P(),
        P(),
        P(),
    )
    return jax.shard_map(
        on_device,
        mesh=mesh,
        in_specs=placed,
        out_specs=(P("dp", None, "space"), P(), P(), P(), P(), P(), P(), P()),
        check_vma=False,
    )
```

```python
import functools
import math

import jax
import jax.numpy as jnp
from jax import lax
from jax.experimental import pallas as pl
from jax.experimental.pallas import tpu as pltpu
from jax.sharding import PartitionSpec as P

SIDE = 8
POOL_ROWS = 16
PACK_ROWS = 24
PART = 256
VMEM = 48 * 1024 * 1024

CUBIC = 0.044715
ROOT_TWO_PI = math.sqrt(2.0 / math.pi)

F32, BF16 = jnp.float32, jnp.bfloat16


def gelu_pair(pre):
    square = pre * pre
    half = 0.5 + 0.5 * jnp.tanh(pre * (ROOT_TWO_PI + (ROOT_TWO_PI * CUBIC) * square))
    value = pre * half
    slope = half + value * (1.0 - half) * (2.0 * ROOT_TWO_PI + (6.0 * ROOT_TWO_PI * CUBIC) * square)
    return value, slope


def mm(left, right):
    return jnp.dot(left, right, preferred_element_type=F32)


def mm_nt(left, right):
    return lax.dot_general(left, right, (((1,), (1,)), ((), ())), preferred_element_type=F32)


def thirds(values):
    high = values.astype(BF16)
    rest = values - high.astype(F32)
    middle = rest.astype(BF16)
    low = (rest - middle.astype(F32)).astype(BF16)
    return jnp.concatenate([high, middle, low], axis=0)


def picked(values, chosen):
    rows = values.shape[0]
    out = mm(thirds(values), chosen)
    return out[:rows] + out[rows : 2 * rows] + out[2 * rows :]


def ones_where(condition):
    return jnp.where(condition, 1.0, 0.0).astype(BF16)


def iota(shape, dim):
    return lax.broadcasted_iota(jnp.int32, shape, dim)


def pack(values):
    tails = jnp.concatenate([values[:8, 128:], values[8:, 128:]], axis=1)
    return jnp.concatenate([values[:, :128], tails], axis=0)


def unpack(packed, blocks):
    tails = packed[POOL_ROWS:]
    tails = jnp.concatenate([tails[:, : blocks - 128], tails[:, blocks - 128 :]], axis=0)
    return jnp.concatenate([packed[:POOL_ROWS], tails], axis=1)


def owners_of(owner_ref, strip, blocks):
    at = strip * blocks
    row = at // 128
    pair = jnp.concatenate([owner_ref[pl.ds(row, 1), :], owner_ref[pl.ds(row + 1, 1), :]], axis=1)
    return jnp.where(at % 128 == 0, pair, pltpu.roll(pair, 256 - blocks % 128, 1))[:, :blocks]


def step_kernel(
    count_all,
    masks,
    *refs,

):
    sent_ref, *got_refs = refs[: len(masks) + 1]
    fields_ref, frac_ref, mask_ref, owner_ref, w1_ref, b1_ref, w2_ref, b2_ref, w3t_ref, b3_ref = refs[
        len(masks) + 1 : len(masks) + 11
    ]
    keep_ref, send_ref, coarse_ref = refs[len(masks) + 11 : len(masks) + 14]
    shifted, weight, w1t, w2t, w2d, w3t, w3p, b3c, pre_one, pre_two, hidden_one, slope_one, hidden_two = refs[
        len(masks) + 14 : len(masks) + 27
    ]
    slope_two, raw_all, scale, d_raw_all, d_two_all, d_one_all, total = refs[len(masks) + 27 :]
    rows, channels, cols = fields_ref.shape
    width = w2_ref.shape[0]
    pools = w3t_ref.shape[0]
    tiles = rows // SIDE
    across = cols // SIDE
    blocks = tiles * across
    taps = 3 * channels
    conv_rows = 3 * taps
    cells = SIDE * cols // 2
    position = lax.axis_index("space")
    core = lax.rem(position, 2)

    def terms(bias):
        high = bias.astype(BF16).astype(F32)
        middle = (bias - high).astype(BF16).astype(F32)
        fill = jnp.zeros((POOL_ROWS - 3, bias.shape[1]), F32)
        return jnp.concatenate([high, middle, bias - high - middle, fill], axis=0)

    def twice(values):
        none = jnp.zeros_like(values)
        return jnp.concatenate(
            [jnp.concatenate([values, none], axis=1), jnp.concatenate([none, values], axis=1)], axis=0
        )

    def doubled(values):
        return jnp.concatenate([values, values], axis=1)

    first_weights, none = w1_ref[...].astype(F32), jnp.zeros((taps, width), F32)
    bias = terms(b1_ref[...])
    w1t[:width, :] = jnp.concatenate([first_weights, none, bias], axis=0).T.astype(BF16)
    w1t[width:, :] = jnp.concatenate([none, first_weights, bias], axis=0).T.astype(BF16)
    second_weights = twice(w2_ref[...].astype(F32))
    w2d[...] = second_weights.astype(BF16)
    w2t[...] = jnp.concatenate([second_weights, doubled(terms(b2_ref[...]))], axis=0).T.astype(BF16)
    last_weights = jnp.concatenate(
        [w3t_ref[...].astype(F32), jnp.zeros((POOL_ROWS - pools, width), F32)], axis=0
    )
    w3t[...] = twice(last_weights).astype(BF16)
    four = twice(twice(last_weights))
    w3p[...] = jnp.concatenate([four, jnp.zeros((128 - 4 * POOL_ROWS, 4 * width), F32)], axis=0).T[
        :, : 4 * POOL_ROWS
    ].astype(BF16)
    bias = jnp.concatenate([b3_ref[...], jnp.zeros((1, width - pools), F32)], axis=1)
    bias = jnp.broadcast_to(bias, (width, width)).T[:POOL_ROWS]
    b3c[...] = jnp.concatenate([bias, bias], axis=0)
    weight[...] = frac_ref[...] * mask_ref[...].astype(F32)

    lane = iota((channels, cols), 1)

    def put(row, values):
        values32 = values.astype(F32)
        left = jnp.where(lane == 0, 0.0, pltpu.roll(values32, 1, 1))
        right = jnp.where(lane == cols - 1, 0.0, pltpu.roll(values32, cols - 1, 1))
        shifted[pl.ds(pl.multiple_of(row * taps, taps), taps), :] = jnp.concatenate(
            [left.astype(BF16), values, right.astype(BF16)], axis=0
        )

    low = high = jnp.zeros((channels, cols), F32)
    for got_ref, mask in zip(got_refs, masks):
        row = got_ref[got_ref.shape[0] - channels :, :]
        low = jnp.where(position ^ mask == position - 1, row, low)
        high = jnp.where(position ^ mask == position + 1, row, high)
    put(0, low.astype(BF16))
    put(rows + 1, high.astype(BF16))

    @pl.loop(0, rows // 8)
    def _(step):
        for inner in range(8):
            put(step * 8 + inner + 1, fields_ref[step * 8 + inner])

    ones = jnp.ones((POOL_ROWS, cells), BF16)

    def taps_of(tile, start, count):
        parts = [
            shifted[pl.ds((tile * SIDE + 2 * (start + i)) * taps, 4 * taps), :]
            for i in range(count)
        ]
        return jnp.concatenate(
            [jnp.concatenate(parts, axis=1), ones[:, : count * cols]], axis=0
        )

    def wide(values, count):
        return jnp.concatenate([values] * count, axis=1)

    parts = [slice(at, at + PART) for at in range(0, cells, PART)]
    pairs = PART // cols

    def first_layer(tile, group):
        here = parts[group]
        pre_one[tile % 2, :, here] = mm(w1t[...], taps_of(tile, group * pairs, pairs))

    for group in range(len(parts)):
        first_layer(0, group)
    halves = (slice(0, width), slice(width, 2 * width))
    for tile in range(tiles):
        now = tile % 2
        for group, here in enumerate(parts):
            if tile + 1 < tiles:
                first_layer(tile + 1, group)
            for rows_of in halves:
                value, slope = gelu_pair(pre_one[now, rows_of, here])
                hidden_one[tile, rows_of, here] = value.astype(BF16)
                slope_one[tile, rows_of, here] = slope
            hidden = jnp.concatenate([hidden_one[tile, :, here], ones[:, :PART]], axis=0)
            pre_two[now, :, here] = mm(w2t[...], hidden)
        if tile > 0:
            raw_all[tile - 1] = mm(w3t[...], hidden_two[tile - 1])
        for here in parts:
            for rows_of in halves:
                value, slope = gelu_pair(pre_two[now, rows_of, here])
                hidden_two[tile, rows_of, here] = value.astype(BF16)
                slope_two[tile, rows_of, here] = slope
    raw_all[tiles - 1] = mm(w3t[...], hidden_two[tiles - 1])

    def over_rows(values):
        both = sum(values[:, i * cols : (i + 1) * cols] for i in range(SIDE // 2))
        return both[:POOL_ROWS] + both[POOL_ROWS:]

    sums = []
    for tile in range(tiles):
        raw = raw_all[tile] + wide(b3c[...], SIDE // 2)
        weights = [
            jnp.broadcast_to(weight[tile * SIDE + i : tile * SIDE + i + 1, :], (POOL_ROWS, cols))
            for i in range(SIDE)
        ]
        weights = jnp.concatenate(
            [jnp.concatenate(weights[i : i + 2], axis=0) for i in range(0, SIDE, 2)], axis=1
        )
        small = jnp.exp(-jnp.abs(raw))
        density = (jnp.maximum(raw, 0.0) + jnp.log1p(small)) * weights
        scale[tile] = jnp.where(raw >= 0.0, 1.0, small) / (1.0 + small) * weights
        sums.append(over_rows(density))
    weight_cols = jnp.sum(weight[...].reshape(tiles, SIDE, cols), axis=1)
    weight_cols = jnp.concatenate([weight_cols, jnp.zeros((-tiles % 8, cols), F32)], axis=0)
    same = ones_where(iota((cols, cols), 0) // SIDE == iota((cols, cols), 1) // SIDE)
    summed = picked(jnp.concatenate(sums + [weight_cols], axis=0), same)
    owners = owners_of(owner_ref, position, blocks)
    target = jnp.zeros((POOL_ROWS, blocks), F32)
    held = [(0, sent_ref, 0)]
    for got_ref, mask in zip(got_refs, masks):
        held = held + [(mask ^ other, got_ref, at) for at, (other, _, _) in enumerate(held)]
    for mask, ref, at in held:
        places = iota((blocks, blocks), 0) + (position ^ mask) * blocks
        packed = ref[at * PACK_ROWS : (at + 1) * PACK_ROWS, :]
        target = target + picked(unpack(packed, blocks), ones_where(places == owners))
    in_tile = iota((blocks, cols), 0) - iota((blocks, cols), 1) // SIDE
    spread = jnp.concatenate([ones_where(in_tile == tile * across) for tile in range(tiles)], axis=1)
    target_cols = picked(target, spread)
    first = iota((cols, blocks), 0)
    in_block = iota((cols, blocks), 1) - first // SIDE
    coarse = jnp.zeros((POOL_ROWS, blocks), F32)
    loss = jnp.zeros((POOL_ROWS, cols), F32)
    valid = iota((POOL_ROWS, cols), 0) < pools
    out_bias = jnp.zeros((POOL_ROWS, cols), F32)
    for tile in range(tiles):
        denom = jnp.maximum(summed[tiles * POOL_ROWS + tile : tiles * POOL_ROWS + tile + 1], 1.0)
        pred = summed[tile * POOL_ROWS : (tile + 1) * POOL_ROWS] / denom
        residual = jnp.where(valid, pred - target_cols[:, tile * cols : (tile + 1) * cols], 0.0)
        loss = loss + residual * residual
        d_cols = residual / (math.sqrt(count_all) * denom)
        d_cols = jnp.concatenate([d_cols, d_cols], axis=0)
        d_raw = (wide(d_cols, SIDE // 2) * scale[tile]).astype(BF16)
        d_raw_all[tile] = d_raw
        out_bias = out_bias + over_rows(d_raw.astype(F32))
        leads = (first % SIDE == 0) & (in_block == tile * across)
        coarse = coarse + picked(pred, ones_where(leads))
    loss = jnp.sum(jnp.sum(loss, axis=1, keepdims=True), axis=0, keepdims=True) * (1.0 / SIDE)
    coarse_rows = pack(coarse)
    coarse_ref[...] = coarse_rows

    mix_at = conv_rows
    out_at = mix_at + width
    bias_at = out_at + POOL_ROWS
    total[...] = jnp.zeros_like(total)

    def to_second(tile):
        d_raw = jnp.concatenate([d_raw_all[tile, :, here] for here in parts], axis=0)
        back = mm(w3p[...], d_raw)
        for group, here in enumerate(parts):
            d_two = back[2 * group * width : 2 * (group + 1) * width] * slope_two[tile, :, here]
            d_two_all[tile % 2, :, here] = d_two.astype(BF16)

    def to_first(tile):
        for here in parts:
            d_one = mm(w2d[...], d_two_all[tile % 2, :, here]) * slope_one[tile, :, here]
            d_one_all[tile % 2, :, here] = d_one.astype(BF16)

    def add_upper(tile):
        got = mm_nt(d_raw_all[tile], hidden_two[tile])
        total[out_at:bias_at, :] += got[:POOL_ROWS, :width] + got[POOL_ROWS:, width:]
        got = mm_nt(jnp.concatenate([hidden_one[tile], ones], axis=0), d_two_all[tile % 2])
        total[mix_at:out_at, :] += got[:width, :width] + got[width : 2 * width, width:]
        extra = got[2 * width : 2 * width + 8]
        total[bias_at + 8 : bias_at + 16, :] += extra[:, :width] + extra[:, width:]

    def add_lower(tile):
        got = mm_nt(taps_of(tile, 0, SIDE // 2), d_one_all[tile % 2])
        total[:conv_rows, :] += got[:conv_rows, :width] + got[taps : taps + conv_rows, width:]
        extra = got[taps + conv_rows : taps + conv_rows + 8]
        total[bias_at : bias_at + 8, :] += extra[:, :width] + extra[:, width:]

    to_second(0)
    to_first(0)
    for tile in range(1, tiles):
        to_second(tile)
        add_upper(tile - 1)
        to_first(tile)
        add_lower(tile - 1)
    add_upper(tiles - 1)
    add_lower(tiles - 1)

    bias = jnp.sum(out_bias, axis=1, keepdims=True)
    here, there = iota((POOL_ROWS, cols), 0), iota((POOL_ROWS, cols), 1)
    bias_row = jnp.sum(jnp.where(here == there, bias, 0.0), axis=0, keepdims=True)
    last = total[out_at:bias_at, :]
    last = jnp.where(here == pools, bias_row, last)
    total[out_at:bias_at, :] = jnp.where(here == pools + 1, loss, last)
    half = keep_ref.shape[0]
    keep_ref[...] = total[pl.ds(pl.multiple_of(core * half, 8), half), :]
    send_ref[:half, :] = total[pl.ds(pl.multiple_of((1 - core) * half, 8), half), :]
    send_ref[half:, :] = coarse_rows


def finish_kernel(
    count_all,
    mine_ref,
    other_ref,
    owner_ref,
    coarse_ref,
    conv_ref,
    conv_bias_ref,
    mix_ref,
    mix_bias_ref,
    out_ref,
    out_bias_ref,
    loss_ref,
):
    position = lax.axis_index("space")
    core = lax.rem(position, 2)
    pools, _, blocks = coarse_ref.shape
    conv_rows, width = conv_ref.shape
    out_at = conv_rows + width
    bias_at = out_at + POOL_ROWS
    half = (bias_at + POOL_ROWS) // 2
    peers = (mine_ref.shape[0] - half) // PACK_ROWS
    mine, other = mine_ref[...], other_ref[...]
    low = jnp.where(core == 0, mine[:half], other[:half])
    high = jnp.where(core == 0, other[:half], mine[:half])
    gathered = jnp.where(core == 1, mine[half:], other[half:])
    total = jnp.concatenate([low, high], axis=0)
    conv_ref[...] = total[:conv_rows]
    mix_ref[...] = total[conv_rows:out_at]
    out_ref[...] = total[out_at : out_at + pools]
    out_bias_ref[...] = total[out_at + pools : out_at + pools + 1, :pools]
    loss_ref[...] = (0.5 / count_all) * total[out_at + pools + 1 : out_at + pools + 2, :1]
    conv_bias_ref[...] = total[bias_at : bias_at + 1]
    mix_bias_ref[...] = total[bias_at + 8 : bias_at + 9]
    base = position | 1
    coarse = jnp.zeros((POOL_ROWS, blocks), F32)
    for peer in range(peers):
        owners = owners_of(owner_ref, base ^ peer, blocks)
        places = iota((blocks, blocks), 0) + position * blocks
        values = unpack(gathered[peer * PACK_ROWS : (peer + 1) * PACK_ROWS], blocks)
        got = mm_nt(thirds(values), ones_where(places == owners))
        coarse = coarse + got[:POOL_ROWS] + got[POOL_ROWS : 2 * POOL_ROWS] + got[2 * POOL_ROWS :]
    coarse_ref[:, 0, :] = coarse[:pools]


def bits_of(size, low):
    return [1 << k for k in range(size.bit_length() - 1) if (1 << k) >= low]


def swapped(values, axis, bit):
    return lax.ppermute(values, axis, [(i, i ^ bit) for i in range(lax.axis_size(axis))])


def crossed(values, step):
    dp, space = lax.axis_size("dp"), lax.axis_size("space")
    dp_moves = [(bit, 0) for bit in bits_of(dp, 1)]
    space_moves = [(0, bit) for bit in bits_of(space, 2)]
    orders = (dp_moves + space_moves, space_moves + dp_moves)
    pairs = []
    for d in range(dp):
        for s in range(space):
            d_bit, s_bit = orders[s % 2][step]
            pairs.append((d * space + s, (d ^ d_bit) * space + (s ^ s_bit)))
    return lax.ppermute(values, ("dp", "space"), pairs)


def reduce_all(keep, send, coarse):
    space = lax.axis_size("space")
    n_dp, n_space = len(bits_of(lax.axis_size("dp"), 1)), len(bits_of(space, 2))
    rows = keep.shape[0]
    got = swapped(send, "space", 1)
    half = keep + got[:rows]
    gathered = jnp.concatenate([coarse, got[rows:]], axis=0)
    for step in range(n_dp + n_space):
        if step < n_space:
            got = crossed(jnp.concatenate([half, gathered], axis=0), step)
            gathered = jnp.concatenate([gathered, got[rows:]], axis=0)
            got = got[:rows]
        else:
            got = crossed(half, step)
        half = half + got
    mine = jnp.concatenate([half, gathered], axis=0)
    return mine, swapped(mine, "space", 1)


def on_device(
    fields,
    land_mask,
    land_frac,
    owner_map,
    targets,
    conv_weight,
    conv_bias,
    mix_weight,
    mix_bias,
    out_weight,
    out_bias,
):
    peers = lax.axis_size("space")
    pools = out_weight.shape[1]
    width = mix_weight.shape[0]
    channels, rows, cols = fields.shape[1:]
    tiles = rows // SIDE
    blocks = tiles * (cols // SIDE)
    count_all = lax.axis_size("dp") * pools * owner_map.shape[0]
    owners = owner_map.reshape(-1, 128)
    position = lax.axis_index("space")
    masks = [2 * bit - 1 for bit in bits_of(peers, 2)] + [1]
    top, bottom = fields[0, :, 0, :].astype(F32), fields[0, :, rows - 1, :].astype(F32)
    held = pack(jnp.pad(targets[0], ((0, POOL_ROWS - pools), (0, 0))))
    gots = []
    for mask in masks:
        payload = jnp.concatenate([held, jnp.where(position ^ mask > position, bottom, top)], axis=0)
        if not gots:
            sent = payload
        got = swapped(payload, "space", mask)
        gots.append(got)
        held = jnp.concatenate([held, got[: held.shape[0]]], axis=0)
    by_row = jnp.swapaxes(fields[0], 0, 1)

    conv_rows = 9 * channels
    half = conv_rows + width + 2 * POOL_ROWS
    half = (half + 31) // 32 * 16
    cells = SIDE * cols // 2
    f32, bf16 = F32, BF16
    keep, send, coarse = pl.pallas_call(
        functools.partial(step_kernel, count_all, masks),
        out_shape=[
            jax.ShapeDtypeStruct((half, width), f32),
            jax.ShapeDtypeStruct((half + PACK_ROWS, width), f32),
            jax.ShapeDtypeStruct((PACK_ROWS, width), f32),
        ],
        in_specs=[pl.BlockSpec(memory_space=pltpu.VMEM)] * (len(masks) + 11),
        out_specs=[pl.BlockSpec(memory_space=pltpu.VMEM)] * 3,
        scratch_shapes=[
            pltpu.VMEM(((rows + 2) * 3 * channels, cols), bf16),
            pltpu.VMEM((rows, cols), f32),
            pltpu.VMEM((2 * width, conv_rows + 3 * channels + POOL_ROWS), bf16),
            pltpu.VMEM((2 * width, 2 * width + POOL_ROWS), bf16),
            pltpu.VMEM((2 * width, 2 * width), bf16),
            pltpu.VMEM((2 * POOL_ROWS, 2 * width), bf16),
            pltpu.VMEM((4 * width, 4 * POOL_ROWS), bf16),
            pltpu.VMEM((2 * POOL_ROWS, cols), f32),
            pltpu.VMEM((2, 2 * width, cells), f32),
            pltpu.VMEM((2, 2 * width, cells), f32),
            pltpu.VMEM((tiles, 2 * width, cells), bf16),
            pltpu.VMEM((tiles, 2 * width, cells), f32),
            pltpu.VMEM((tiles, 2 * width, cells), bf16),
            pltpu.VMEM((tiles, 2 * width, cells), f32),
            pltpu.VMEM((tiles, 2 * POOL_ROWS, cells), f32),
            pltpu.VMEM((tiles, 2 * POOL_ROWS, cells), f32),
            pltpu.VMEM((tiles, 2 * POOL_ROWS, cells), bf16),
            pltpu.VMEM((2, 2 * width, cells), bf16),
            pltpu.VMEM((2, 2 * width, cells), bf16),
            pltpu.VMEM((2 * half, width), f32),
        ],
        compiler_params=pltpu.CompilerParams(vmem_limit_bytes=VMEM),
        name="train_step",
    )(
        sent,
        *gots,
        by_row,
        land_frac,
        land_mask,
        owners,
        conv_weight.reshape(conv_rows, width),
        conv_bias.reshape(1, width),
        mix_weight,
        mix_bias.reshape(1, width),
        out_weight.T,
        out_bias.reshape(1, pools),
    )
    mine, other = reduce_all(keep, send, coarse)
    outs = pl.pallas_call(
        functools.partial(finish_kernel, count_all),
        out_shape=[
            jax.ShapeDtypeStruct((pools, 1, blocks), f32),
            jax.ShapeDtypeStruct((conv_rows, width), f32),
            jax.ShapeDtypeStruct((1, width), f32),
            jax.ShapeDtypeStruct((width, width), f32),
            jax.ShapeDtypeStruct((1, width), f32),
            jax.ShapeDtypeStruct((pools, width), f32),
            jax.ShapeDtypeStruct((1, pools), f32),
            jax.ShapeDtypeStruct((1, 1), f32),
        ],
        in_specs=[pl.BlockSpec(memory_space=pltpu.VMEM)] * 3,
        out_specs=[pl.BlockSpec(memory_space=pltpu.VMEM)] * 8,
        compiler_params=pltpu.CompilerParams(vmem_limit_bytes=VMEM),
        name="finish",
    )(mine, other, owners)
    coarse_pred, conv_grad, conv_bias_grad, mix_grad, mix_bias_grad, out_grad, out_bias_grad, loss = outs
    return (
        jnp.swapaxes(coarse_pred, 0, 1),
        conv_grad.reshape(conv_weight.shape),
        conv_bias_grad.reshape(width),
        mix_grad,
        mix_bias_grad.reshape(width),
        out_grad.T,
        out_bias_grad.reshape(pools),
        loss.reshape(()),
    )


def solution(mesh):
    placed = (
        P("dp", None, "space", None),
        P("space", None),
        P("space", None),
        P(),
        P("dp", None, "space"),
        P(),
        P(),
        P(),
        P(),
        P(),
        P(),
    )
    return jax.shard_map(
        on_device,
        mesh=mesh,
        in_specs=placed,
        out_specs=(P("dp", None, "space"), P(), P(), P(), P(), P(), P(), P()),
        check_vma=False,
    )
```

```python
import functools
import math

import jax
import jax.numpy as jnp
from jax import lax
from jax.experimental import pallas as pl
from jax.experimental.pallas import tpu as pltpu
from jax.sharding import PartitionSpec as P

SIDE = 8
POOL_ROWS = 16
PACK_ROWS = 24
PART = 256
VMEM = 46 * 1024 * 1024
PREPARE_VMEM = 8 * 1024 * 1024

CUBIC = 0.044715
ROOT_TWO_PI = math.sqrt(2.0 / math.pi)

F32, BF16 = jnp.float32, jnp.bfloat16


def gelu_pair(pre):
    square = pre * pre
    half = 0.5 + 0.5 * jnp.tanh(pre * (ROOT_TWO_PI + (ROOT_TWO_PI * CUBIC) * square))
    value = pre * half
    slope = half + value * (1.0 - half) * (2.0 * ROOT_TWO_PI + (6.0 * ROOT_TWO_PI * CUBIC) * square)
    return value, slope


def mm(left, right):
    return jnp.dot(left, right, preferred_element_type=F32)


def mm_nt(left, right):
    return lax.dot_general(left, right, (((1,), (1,)), ((), ())), preferred_element_type=F32)


def thirds(values):
    high = values.astype(BF16)
    rest = values - high.astype(F32)
    middle = rest.astype(BF16)
    low = (rest - middle.astype(F32)).astype(BF16)
    return jnp.concatenate([high, middle, low], axis=0)


def picked(values, chosen):
    rows = values.shape[0]
    out = mm(thirds(values), chosen)
    return out[:rows] + out[rows : 2 * rows] + out[2 * rows :]


def ones_where(condition):
    return jnp.where(condition, 1.0, 0.0).astype(BF16)


def iota(shape, dim):
    return lax.broadcasted_iota(jnp.int32, shape, dim)


def pack(values):
    tails = jnp.concatenate([values[:8, 128:], values[8:, 128:]], axis=1)
    return jnp.concatenate([values[:, :128], tails], axis=0)


def unpack(packed, blocks):
    tails = packed[POOL_ROWS:]
    tails = jnp.concatenate([tails[:, : blocks - 128], tails[:, blocks - 128 :]], axis=0)
    return jnp.concatenate([packed[:POOL_ROWS], tails], axis=1)


def owners_of(owner_ref, strip, blocks):
    at = strip * blocks
    row = at // 128
    pair = jnp.concatenate([owner_ref[pl.ds(row, 1), :], owner_ref[pl.ds(row + 1, 1), :]], axis=1)
    return jnp.where(at % 128 == 0, pair, pltpu.roll(pair, 256 - blocks % 128, 1))[:, :blocks]


def three_taps(row):
    lane = iota(row.shape, 1)
    last = row.shape[1] - 1
    left = jnp.where(lane == 0, 0.0, pltpu.roll(row, 1, 1))
    right = jnp.where(lane == last, 0.0, pltpu.roll(row, last, 1))
    return jnp.concatenate([left, row, right], axis=0).astype(BF16)


def pack_kernel(masks, top_ref, bottom_ref, target_ref, sent_ref, rows_ref):
    position = lax.axis_index("space")
    pools, _, blocks = target_ref.shape
    channels = top_ref.shape[1]
    edge = bottom_ref.shape[2] - 1
    top = top_ref[0].astype(F32)[:, 0, :]
    bottom = bottom_ref[0].astype(F32)[:, edge, :]
    values = jnp.concatenate(
        [target_ref[:, 0, :], jnp.zeros((POOL_ROWS - pools, blocks), F32)], axis=0
    )
    sent_ref[:PACK_ROWS, :] = pack(values)
    for at, mask in enumerate(masks):
        row = jnp.where(position ^ mask > position, bottom, top)
        rows_ref[at] = row
        if at == 0:
            sent_ref[PACK_ROWS:, :] = row


def prepare_kernel(
    fields_ref,
    frac_ref,
    mask_ref,
    w1_ref,
    b1_ref,
    w2_ref,
    b2_ref,
    w3t_ref,
    b3_ref,
    shifted,
    weight,
    w1t,
    w2t,
    w2d,
    w3t,
    w3p,
    b3c,
):
    rows, channels, cols = fields_ref.shape
    width = w2_ref.shape[0]
    pools = w3t_ref.shape[0]
    taps = 3 * channels

    def terms(bias):
        high = bias.astype(BF16).astype(F32)
        middle = (bias - high).astype(BF16).astype(F32)
        fill = jnp.zeros((POOL_ROWS - 3, bias.shape[1]), F32)
        return jnp.concatenate([high, middle, bias - high - middle, fill], axis=0)

    def twice(values):
        none = jnp.zeros_like(values)
        return jnp.concatenate(
            [jnp.concatenate([values, none], axis=1), jnp.concatenate([none, values], axis=1)], axis=0
        )

    def doubled(values):
        return jnp.concatenate([values, values], axis=1)

    first_weights, none = w1_ref[...].astype(F32), jnp.zeros((taps, width), F32)
    bias = terms(b1_ref[...])
    w1t[:width, :] = jnp.concatenate([first_weights, none, bias], axis=0).T.astype(BF16)
    w1t[width:, :] = jnp.concatenate([none, first_weights, bias], axis=0).T.astype(BF16)
    second_weights = twice(w2_ref[...].astype(F32))
    w2d[...] = second_weights.astype(BF16)
    w2t[...] = jnp.concatenate([second_weights, doubled(terms(b2_ref[...]))], axis=0).T.astype(BF16)
    last_weights = jnp.concatenate(
        [w3t_ref[...].astype(F32), jnp.zeros((POOL_ROWS - pools, width), F32)], axis=0
    )
    w3t[...] = twice(last_weights).astype(BF16)
    four = twice(twice(last_weights))
    w3p[...] = jnp.concatenate([four, jnp.zeros((128 - 4 * POOL_ROWS, 4 * width), F32)], axis=0).T[
        :, : 4 * POOL_ROWS
    ].astype(BF16)
    bias = jnp.concatenate([b3_ref[...], jnp.zeros((1, width - pools), F32)], axis=1)
    bias = jnp.broadcast_to(bias, (width, width)).T[:POOL_ROWS]
    b3c[...] = jnp.concatenate([bias, bias], axis=0)
    weight[...] = frac_ref[...] * mask_ref[...].astype(F32)

    for row in range(rows):
        shifted[row * taps : (row + 1) * taps, :] = three_taps(fields_ref[row].astype(F32))


def step_kernel(
    count_all,
    masks,
    pools,
    *refs,

):
    sent_ref, *got_refs = refs[: len(masks) + 1]
    owner_ref, shifted, weight, w1t, w2t, w2d, w3t, w3p, b3c = refs[len(masks) + 1 : len(masks) + 10]
    keep_ref, send_ref, coarse_ref = refs[len(masks) + 10 : len(masks) + 13]
    lower, upper, pre_one, pre_two, hidden_one, slope_one, hidden_two, slope_two = refs[
        len(masks) + 13 : len(masks) + 21
    ]
    raw_all, scale, d_raw_all, d_two_all, d_one_all, total = refs[len(masks) + 21 :]
    rows, cols = weight.shape
    channels = lower.shape[0] // 12
    width = w2d.shape[0] // 2
    tiles = rows // SIDE
    across = cols // SIDE
    blocks = tiles * across
    taps = 3 * channels
    conv_rows = 3 * taps
    cells = SIDE * cols // 2
    position = lax.axis_index("space")
    core = lax.rem(position, 2)

    low = high = jnp.zeros((channels, cols), F32)
    for got_ref, mask in zip(got_refs, masks):
        row = got_ref[got_ref.shape[0] - channels :, :]
        low = jnp.where(position ^ mask == position - 1, row, low)
        high = jnp.where(position ^ mask == position + 1, row, high)
    lower[:taps, :] = three_taps(low)
    lower[taps:, :] = shifted[:conv_rows, :]
    upper[:conv_rows, :] = shifted[rows * taps - conv_rows :, :]
    upper[conv_rows:, :] = three_taps(high)

    ones = jnp.ones((POOL_ROWS, cells), BF16)

    def taps_of(tile, start, count):
        parts = []
        for i in range(start, start + count):
            row = tile * SIDE + 2 * i - 1
            if row < 0:
                parts.append(lower[...])
            elif row + 4 > rows:
                parts.append(upper[...])
            else:
                parts.append(shifted[row * taps : (row + 4) * taps, :])
        return jnp.concatenate(
            [jnp.concatenate(parts, axis=1), ones[:, : count * cols]], axis=0
        )

    def wide(values, count):
        return jnp.concatenate([values] * count, axis=1)

    parts = [slice(at, at + PART) for at in range(0, cells, PART)]
    pairs = PART // cols

    def first_layer(tile, group):
        here = parts[group]
        pre_one[tile % 2, :, here] = mm(w1t[...], taps_of(tile, group * pairs, pairs))

    for group in range(len(parts)):
        first_layer(0, group)
    halves = (slice(0, width), slice(width, 2 * width))
    for tile in range(tiles):
        now = tile % 2
        for group, here in enumerate(parts):
            if tile + 1 < tiles:
                first_layer(tile + 1, group)
            for rows_of in halves:
                value, slope = gelu_pair(pre_one[now, rows_of, here])
                hidden_one[tile, rows_of, here] = value.astype(BF16)
                slope_one[tile, rows_of, here] = slope
            hidden = jnp.concatenate([hidden_one[tile, :, here], ones[:, :PART]], axis=0)
            pre_two[now, :, here] = mm(w2t[...], hidden)
        if tile > 0:
            raw_all[tile - 1] = mm(w3t[...], hidden_two[tile - 1])
        for here in parts:
            for rows_of in halves:
                value, slope = gelu_pair(pre_two[now, rows_of, here])
                hidden_two[tile, rows_of, here] = value.astype(BF16)
                slope_two[tile, rows_of, here] = slope
    raw_all[tiles - 1] = mm(w3t[...], hidden_two[tiles - 1])

    def over_rows(values):
        both = sum(values[:, i * cols : (i + 1) * cols] for i in range(SIDE // 2))
        return both[:POOL_ROWS] + both[POOL_ROWS:]

    sums = []
    for tile in range(tiles):
        raw = raw_all[tile] + wide(b3c[...], SIDE // 2)
        weights = [
            jnp.broadcast_to(weight[tile * SIDE + i : tile * SIDE + i + 1, :], (POOL_ROWS, cols))
            for i in range(SIDE)
        ]
        weights = jnp.concatenate(
            [jnp.concatenate(weights[i : i + 2], axis=0) for i in range(0, SIDE, 2)], axis=1
        )
        small = jnp.exp(-jnp.abs(raw))
        density = (jnp.maximum(raw, 0.0) + jnp.log1p(small)) * weights
        scale[tile] = jnp.where(raw >= 0.0, 1.0, small) / (1.0 + small) * weights
        sums.append(over_rows(density))
    weight_cols = jnp.sum(weight[...].reshape(tiles, SIDE, cols), axis=1)
    weight_cols = jnp.concatenate([weight_cols, jnp.zeros((-tiles % 8, cols), F32)], axis=0)
    same = ones_where(iota((cols, cols), 0) // SIDE == iota((cols, cols), 1) // SIDE)
    summed = picked(jnp.concatenate(sums + [weight_cols], axis=0), same)
    owners = owners_of(owner_ref, position, blocks)
    target = jnp.zeros((POOL_ROWS, blocks), F32)
    held = [(0, sent_ref, 0)]
    for got_ref, mask in zip(got_refs, masks):
        held = held + [(mask ^ other, got_ref, at) for at, (other, _, _) in enumerate(held)]
    for mask, ref, at in held:
        places = iota((blocks, blocks), 0) + (position ^ mask) * blocks
        packed = ref[at * PACK_ROWS : (at + 1) * PACK_ROWS, :]
        target = target + picked(unpack(packed, blocks), ones_where(places == owners))
    in_tile = iota((blocks, cols), 0) - iota((blocks, cols), 1) // SIDE
    spread = jnp.concatenate([ones_where(in_tile == tile * across) for tile in range(tiles)], axis=1)
    target_cols = picked(target, spread)
    first = iota((cols, blocks), 0)
    in_block = iota((cols, blocks), 1) - first // SIDE
    coarse = jnp.zeros((POOL_ROWS, blocks), F32)
    loss = jnp.zeros((POOL_ROWS, cols), F32)
    valid = iota((POOL_ROWS, cols), 0) < pools
    out_bias = jnp.zeros((POOL_ROWS, cols), F32)
    for tile in range(tiles):
        denom = jnp.maximum(summed[tiles * POOL_ROWS + tile : tiles * POOL_ROWS + tile + 1], 1.0)
        pred = summed[tile * POOL_ROWS : (tile + 1) * POOL_ROWS] / denom
        residual = jnp.where(valid, pred - target_cols[:, tile * cols : (tile + 1) * cols], 0.0)
        loss = loss + residual * residual
        d_cols = residual / (math.sqrt(count_all) * denom)
        d_cols = jnp.concatenate([d_cols, d_cols], axis=0)
        d_raw = (wide(d_cols, SIDE // 2) * scale[tile]).astype(BF16)
        d_raw_all[tile] = d_raw
        out_bias = out_bias + over_rows(d_raw.astype(F32))
        leads = (first % SIDE == 0) & (in_block == tile * across)
        coarse = coarse + picked(pred, ones_where(leads))
    loss = jnp.sum(jnp.sum(loss, axis=1, keepdims=True), axis=0, keepdims=True) * (1.0 / SIDE)
    coarse_rows = pack(coarse)
    coarse_ref[...] = coarse_rows

    mix_at = conv_rows
    out_at = mix_at + width
    bias_at = out_at + POOL_ROWS
    total[...] = jnp.zeros_like(total)

    def to_second(tile):
        d_raw = jnp.concatenate([d_raw_all[tile, :, here] for here in parts], axis=0)
        back = mm(w3p[...], d_raw)
        for group, here in enumerate(parts):
            d_two = back[2 * group * width : 2 * (group + 1) * width] * slope_two[tile, :, here]
            d_two_all[tile % 2, :, here] = d_two.astype(BF16)

    def to_first(tile):
        for here in parts:
            d_one = mm(w2d[...], d_two_all[tile % 2, :, here]) * slope_one[tile, :, here]
            d_one_all[tile % 2, :, here] = d_one.astype(BF16)

    def add_upper(tile):
        got = mm_nt(d_raw_all[tile], hidden_two[tile])
        total[out_at:bias_at, :] += got[:POOL_ROWS, :width] + got[POOL_ROWS:, width:]
        got = mm_nt(jnp.concatenate([hidden_one[tile], ones], axis=0), d_two_all[tile % 2])
        total[mix_at:out_at, :] += got[:width, :width] + got[width : 2 * width, width:]
        extra = got[2 * width : 2 * width + 8]
        total[bias_at + 8 : bias_at + 16, :] += extra[:, :width] + extra[:, width:]

    def add_lower(tile):
        got = mm_nt(taps_of(tile, 0, SIDE // 2), d_one_all[tile % 2])
        total[:conv_rows, :] += got[:conv_rows, :width] + got[taps : taps + conv_rows, width:]
        extra = got[taps + conv_rows : taps + conv_rows + 8]
        total[bias_at : bias_at + 8, :] += extra[:, :width] + extra[:, width:]

    to_second(0)
    to_first(0)
    for tile in range(1, tiles):
        to_second(tile)
        add_upper(tile - 1)
        to_first(tile)
        add_lower(tile - 1)
    add_upper(tiles - 1)
    add_lower(tiles - 1)

    bias = jnp.sum(out_bias, axis=1, keepdims=True)
    here, there = iota((POOL_ROWS, cols), 0), iota((POOL_ROWS, cols), 1)
    bias_row = jnp.sum(jnp.where(here == there, bias, 0.0), axis=0, keepdims=True)
    last = total[out_at:bias_at, :]
    last = jnp.where(here == pools, bias_row, last)
    total[out_at:bias_at, :] = jnp.where(here == pools + 1, loss, last)
    half = keep_ref.shape[0]
    keep_ref[...] = total[pl.ds(pl.multiple_of(core * half, 8), half), :]
    send_ref[:half, :] = total[pl.ds(pl.multiple_of((1 - core) * half, 8), half), :]
    send_ref[half:, :] = coarse_rows


def finish_kernel(
    count_all,
    mine_ref,
    other_ref,
    owner_ref,
    coarse_ref,
    conv_ref,
    conv_bias_ref,
    mix_ref,
    mix_bias_ref,
    out_ref,
    out_bias_ref,
    loss_ref,
):
    position = lax.axis_index("space")
    core = lax.rem(position, 2)
    pools, _, blocks = coarse_ref.shape
    conv_rows, width = conv_ref.shape
    out_at = conv_rows + width
    bias_at = out_at + POOL_ROWS
    half = (bias_at + POOL_ROWS) // 2
    peers = (mine_ref.shape[0] - half) // PACK_ROWS
    mine, other = mine_ref[...], other_ref[...]
    low = jnp.where(core == 0, mine[:half], other[:half])
    high = jnp.where(core == 0, other[:half], mine[:half])
    gathered = jnp.where(core == 1, mine[half:], other[half:])
    total = jnp.concatenate([low, high], axis=0)
    conv_ref[...] = total[:conv_rows]
    mix_ref[...] = total[conv_rows:out_at]
    out_ref[...] = total[out_at : out_at + pools]
    out_bias_ref[...] = total[out_at + pools : out_at + pools + 1, :pools]
    loss_ref[...] = (0.5 / count_all) * total[out_at + pools + 1 : out_at + pools + 2, :1]
    conv_bias_ref[...] = total[bias_at : bias_at + 1]
    mix_bias_ref[...] = total[bias_at + 8 : bias_at + 9]
    base = position | 1
    coarse = jnp.zeros((POOL_ROWS, blocks), F32)
    for peer in range(peers):
        owners = owners_of(owner_ref, base ^ peer, blocks)
        places = iota((blocks, blocks), 0) + position * blocks
        values = unpack(gathered[peer * PACK_ROWS : (peer + 1) * PACK_ROWS], blocks)
        got = mm_nt(thirds(values), ones_where(places == owners))
        coarse = coarse + got[:POOL_ROWS] + got[POOL_ROWS : 2 * POOL_ROWS] + got[2 * POOL_ROWS :]
    coarse_ref[:, 0, :] = coarse[:pools]


def bits_of(size, low):
    return [1 << k for k in range(size.bit_length() - 1) if (1 << k) >= low]


def swapped(values, axis, bit):
    return lax.ppermute(values, axis, [(i, i ^ bit) for i in range(lax.axis_size(axis))])


def crossed(values, step):
    dp, space = lax.axis_size("dp"), lax.axis_size("space")
    dp_moves = [(bit, 0) for bit in bits_of(dp, 1)]
    space_moves = [(0, bit) for bit in bits_of(space, 2)]
    orders = (dp_moves + space_moves, space_moves + dp_moves)
    pairs = []
    for d in range(dp):
        for s in range(space):
            d_bit, s_bit = orders[s % 2][step]
            pairs.append((d * space + s, (d ^ d_bit) * space + (s ^ s_bit)))
    return lax.ppermute(values, ("dp", "space"), pairs)


def reduce_all(keep, send, coarse):
    space = lax.axis_size("space")
    n_dp, n_space = len(bits_of(lax.axis_size("dp"), 1)), len(bits_of(space, 2))
    rows = keep.shape[0]
    got = swapped(send, "space", 1)
    half = keep + got[:rows]
    gathered = jnp.concatenate([coarse, got[rows:]], axis=0)
    for step in range(n_dp + n_space):
        if step < n_space:
            got = crossed(jnp.concatenate([half, gathered], axis=0), step)
            gathered = jnp.concatenate([gathered, got[rows:]], axis=0)
            got = got[:rows]
        else:
            got = crossed(half, step)
        half = half + got
    mine = jnp.concatenate([half, gathered], axis=0)
    return mine, swapped(mine, "space", 1)


def on_device(
    fields,
    land_mask,
    land_frac,
    owner_map,
    targets,
    conv_weight,
    conv_bias,
    mix_weight,
    mix_bias,
    out_weight,
    out_bias,
):
    peers = lax.axis_size("space")
    pools = out_weight.shape[1]
    width = mix_weight.shape[0]
    channels, rows, cols = fields.shape[1:]
    tiles = rows // SIDE
    blocks = tiles * (cols // SIDE)
    count_all = lax.axis_size("dp") * pools * owner_map.shape[0]
    owners = owner_map.reshape(-1, 128)
    position = lax.axis_index("space")
    masks = [2 * bit - 1 for bit in bits_of(peers, 2)] + [1]
    sent, edges = pl.pallas_call(
        functools.partial(pack_kernel, masks),
        out_shape=[
            jax.ShapeDtypeStruct((PACK_ROWS + channels, cols), F32),
            jax.ShapeDtypeStruct((len(masks), channels, cols), F32),
        ],
        grid=(1,),
        in_specs=[
            pl.BlockSpec((1, channels, 16, cols), lambda i: (0, 0, 0, 0)),
            pl.BlockSpec((1, channels, 16, cols), lambda i: (0, 0, rows // 16 - 1, 0)),
            pl.BlockSpec((pools, 1, blocks), lambda i: (0, 0, 0)),
        ],
        name="pack_edges",
    )(fields, fields, jnp.swapaxes(targets, 0, 1))
    payload, gots = sent, []
    for at, mask in enumerate(masks):
        if at > 0:
            payload = jnp.concatenate([held, edges[at]], axis=0)
        got = swapped(payload, "space", mask)
        gots.append(got)
        had = payload.shape[0] - channels
        held = jnp.concatenate([payload[:had], got[:had]], axis=0)
    later, _ = lax.optimization_barrier((fields, sent))
    by_row = jnp.swapaxes(later[0], 0, 1)
    by_row, _ = lax.optimization_barrier((by_row, gots[0]))

    conv_rows = 9 * channels
    half = conv_rows + width + 2 * POOL_ROWS
    half = (half + 31) // 32 * 16
    cells = SIDE * cols // 2
    f32, bf16 = F32, BF16
    prepared = pl.pallas_call(
        prepare_kernel,
        out_shape=[
            pltpu.VMEM((rows * 3 * channels, cols), bf16),
            pltpu.VMEM((rows, cols), f32),
            pltpu.VMEM((2 * width, conv_rows + 3 * channels + POOL_ROWS), bf16),
            pltpu.VMEM((2 * width, 2 * width + POOL_ROWS), bf16),
            pltpu.VMEM((2 * width, 2 * width), bf16),
            pltpu.VMEM((2 * POOL_ROWS, 2 * width), bf16),
            pltpu.VMEM((4 * width, 4 * POOL_ROWS), bf16),
            pltpu.VMEM((2 * POOL_ROWS, cols), f32),
        ],
        in_specs=[pl.BlockSpec(memory_space=pltpu.VMEM)] * 9,
        out_specs=[pl.BlockSpec(memory_space=pltpu.VMEM)] * 8,
        compiler_params=pltpu.CompilerParams(vmem_limit_bytes=PREPARE_VMEM),
        cost_estimate=pl.CostEstimate(flops=10**9, bytes_accessed=4 * 10**6, transcendentals=0),
        name="prepare",
    )(
        by_row,
        land_frac,
        land_mask,
        conv_weight.reshape(conv_rows, width),
        conv_bias.reshape(1, width),
        mix_weight,
        mix_bias.reshape(1, width),
        out_weight.T,
        out_bias.reshape(1, pools),
    )
    keep, send, coarse = pl.pallas_call(
        functools.partial(step_kernel, count_all, masks, pools),
        out_shape=[
            jax.ShapeDtypeStruct((half, width), f32),
            jax.ShapeDtypeStruct((half + PACK_ROWS, width), f32),
            jax.ShapeDtypeStruct((PACK_ROWS, width), f32),
        ],
        in_specs=[pl.BlockSpec(memory_space=pltpu.VMEM)] * (len(masks) + 10),
        out_specs=[pl.BlockSpec(memory_space=pltpu.VMEM)] * 3,
        scratch_shapes=[
            pltpu.VMEM((12 * channels, cols), bf16),
            pltpu.VMEM((12 * channels, cols), bf16),
            pltpu.VMEM((2, 2 * width, cells), f32),
            pltpu.VMEM((2, 2 * width, cells), f32),
            pltpu.VMEM((tiles, 2 * width, cells), bf16),
            pltpu.VMEM((tiles, 2 * width, cells), f32),
            pltpu.VMEM((tiles, 2 * width, cells), bf16),
            pltpu.VMEM((tiles, 2 * width, cells), f32),
            pltpu.VMEM((tiles, 2 * POOL_ROWS, cells), f32),
            pltpu.VMEM((tiles, 2 * POOL_ROWS, cells), f32),
            pltpu.VMEM((tiles, 2 * POOL_ROWS, cells), bf16),
            pltpu.VMEM((2, 2 * width, cells), bf16),
            pltpu.VMEM((2, 2 * width, cells), bf16),
            pltpu.VMEM((2 * half, width), f32),
        ],
        compiler_params=pltpu.CompilerParams(vmem_limit_bytes=VMEM),
        name="train_step",
    )(
        sent,
        *gots,
        owners,
        *prepared,
    )
    mine, other = reduce_all(keep, send, coarse)
    outs = pl.pallas_call(
        functools.partial(finish_kernel, count_all),
        out_shape=[
            jax.ShapeDtypeStruct((pools, 1, blocks), f32),
            jax.ShapeDtypeStruct((conv_rows, width), f32),
            jax.ShapeDtypeStruct((1, width), f32),
            jax.ShapeDtypeStruct((width, width), f32),
            jax.ShapeDtypeStruct((1, width), f32),
            jax.ShapeDtypeStruct((pools, width), f32),
            jax.ShapeDtypeStruct((1, pools), f32),
            jax.ShapeDtypeStruct((1, 1), f32),
        ],
        in_specs=[pl.BlockSpec(memory_space=pltpu.VMEM)] * 3,
        out_specs=[pl.BlockSpec(memory_space=pltpu.VMEM)] * 8,
        compiler_params=pltpu.CompilerParams(vmem_limit_bytes=VMEM),
        name="finish",
    )(mine, other, owners)
    coarse_pred, conv_grad, conv_bias_grad, mix_grad, mix_bias_grad, out_grad, out_bias_grad, loss = outs
    return (
        jnp.swapaxes(coarse_pred, 0, 1),
        conv_grad.reshape(conv_weight.shape),
        conv_bias_grad.reshape(width),
        mix_grad,
        mix_bias_grad.reshape(width),
        out_grad.T,
        out_bias_grad.reshape(pools),
        loss.reshape(()),
    )


def solution(mesh):
    placed = (
        P("dp", None, "space", None),
        P("space", None),
        P("space", None),
        P(),
        P("dp", None, "space"),
        P(),
        P(),
        P(),
        P(),
        P(),
        P(),
    )
    return jax.shard_map(
        on_device,
        mesh=mesh,
        in_specs=placed,
        out_specs=(P("dp", None, "space"), P(), P(), P(), P(), P(), P(), P()),
        check_vma=False,
    )
```

```python
import functools
import math

import jax
import jax.numpy as jnp
from jax import lax
from jax.experimental import pallas as pl
from jax.experimental.pallas import tpu as pltpu
from jax.sharding import PartitionSpec as P

SIDE = 8
POOL_ROWS = 16
PACK_ROWS = 24
PART = 256
VMEM = 46 * 1024 * 1024
PREPARE_VMEM = 8 * 1024 * 1024
ALL_VMEM = 127 * 512 * 1024

CUBIC = 0.044715
ROOT_TWO_PI = math.sqrt(2.0 / math.pi)

F32, BF16 = jnp.float32, jnp.bfloat16


def gelu_pair(half):
    square = half * half
    tanh_value = jnp.tanh(half * (2.0 * ROOT_TWO_PI + (8.0 * ROOT_TWO_PI * CUBIC) * square))
    above = 1.0 + tanh_value
    value = half * above
    slope = above + value * (1.0 - tanh_value) * (2.0 * ROOT_TWO_PI + (24.0 * ROOT_TWO_PI * CUBIC) * square)
    return value, slope


def mm(left, right):
    return jnp.dot(left, right, preferred_element_type=F32)


def mm_nt(left, right):
    return lax.dot_general(left, right, (((1,), (1,)), ((), ())), preferred_element_type=F32)


def thirds(values):
    high = values.astype(BF16)
    rest = values - high.astype(F32)
    middle = rest.astype(BF16)
    low = (rest - middle.astype(F32)).astype(BF16)
    return jnp.concatenate([high, middle, low], axis=0)


def picked(values, chosen):
    rows = values.shape[0]
    out = mm(thirds(values), chosen)
    return out[:rows] + out[rows : 2 * rows] + out[2 * rows :]


def ones_where(condition):
    return jnp.where(condition, 1.0, 0.0).astype(BF16)


def iota(shape, dim):
    return lax.broadcasted_iota(jnp.int32, shape, dim)


def pack(values):
    tails = jnp.concatenate([values[:8, 128:], values[8:, 128:]], axis=1)
    return jnp.concatenate([values[:, :128], tails], axis=0)


def unpack(packed, blocks):
    tails = packed[POOL_ROWS:]
    tails = jnp.concatenate([tails[:, : blocks - 128], tails[:, blocks - 128 :]], axis=0)
    return jnp.concatenate([packed[:POOL_ROWS], tails], axis=1)


def owners_of(owner_ref, strip, blocks):
    at = strip * blocks
    row = at // 128
    pair = jnp.concatenate([owner_ref[pl.ds(row, 1), :], owner_ref[pl.ds(row + 1, 1), :]], axis=1)
    return jnp.where(at % 128 == 0, pair, pltpu.roll(pair, 256 - blocks % 128, 1))[:, :blocks]


def three_taps(row):
    lane = iota(row.shape, 1)
    last = row.shape[1] - 1
    left = jnp.where(lane == 0, 0.0, pltpu.roll(row, 1, 1))
    right = jnp.where(lane == last, 0.0, pltpu.roll(row, last, 1))
    return jnp.concatenate([left, row, right], axis=0).astype(BF16)


def pack_kernel(
    fields_ref, target_ref, sent_ref, outer_ref, inner_ref, top_rows, bottom_rows, targets, done
):
    rows, some = fields_ref.shape[2], top_rows.shape[1]
    copies = [
        pltpu.make_async_copy(fields_ref.at[0, :, pl.ds(0, some), :], top_rows, done.at[0]),
        pltpu.make_async_copy(fields_ref.at[0, :, pl.ds(rows - some, some), :], bottom_rows, done.at[1]),
        pltpu.make_async_copy(target_ref, targets, done.at[2]),
    ]
    for copy in copies:
        copy.start()
    for copy in copies:
        copy.wait()
    core = lax.rem(lax.axis_index("space"), 2)
    pools, _, blocks = target_ref.shape
    top = top_rows[...].astype(F32)[:, 0, :]
    bottom = bottom_rows[...].astype(F32)[:, some - 1, :]
    values = jnp.concatenate(
        [targets[:, 0, :], jnp.zeros((POOL_ROWS - pools, blocks), F32)], axis=0
    )
    sent_ref[:PACK_ROWS, :] = pack(values)
    sent_ref[PACK_ROWS:, :] = jnp.where(core == 0, top, bottom)
    outer_ref[...] = jnp.where(core == 0, top, bottom)
    inner_ref[...] = jnp.where(core == 0, bottom, top)


def prepare_kernel(
    fields_ref,
    frac_ref,
    mask_ref,
    w1_ref,
    b1_ref,
    w2_ref,
    b2_ref,
    w3t_ref,
    b3_ref,
    owner_ref,
    shifted,
    weight,
    owners,
    w1t,
    w2t,
    w2d,
    w3t,
    w3p,
    b3c,
):
    rows, channels, cols = fields_ref.shape
    width = w2_ref.shape[0]
    pools = w3t_ref.shape[0]
    taps = 3 * channels

    def terms(bias):
        high = bias.astype(BF16).astype(F32)
        middle = (bias - high).astype(BF16).astype(F32)
        fill = jnp.zeros((POOL_ROWS - 3, bias.shape[1]), F32)
        return jnp.concatenate([high, middle, bias - high - middle, fill], axis=0)

    def twice(values):
        none = jnp.zeros_like(values)
        return jnp.concatenate(
            [jnp.concatenate([values, none], axis=1), jnp.concatenate([none, values], axis=1)], axis=0
        )

    def doubled(values):
        return jnp.concatenate([values, values], axis=1)

    first_weights, none = 0.5 * w1_ref[...].astype(F32), jnp.zeros((taps, width), F32)
    bias = terms(0.5 * b1_ref[...])
    w1t[:width, :] = jnp.concatenate([first_weights, none, bias], axis=0).T.astype(BF16)
    w1t[width:, :] = jnp.concatenate([none, first_weights, bias], axis=0).T.astype(BF16)
    second_weights = twice(0.5 * w2_ref[...].astype(F32))
    w2d[...] = second_weights.astype(BF16)
    w2t[...] = jnp.concatenate([second_weights, doubled(terms(0.5 * b2_ref[...]))], axis=0).T.astype(BF16)
    last_weights = jnp.concatenate(
        [w3t_ref[...].astype(F32), jnp.zeros((POOL_ROWS - pools, width), F32)], axis=0
    )
    w3t[...] = twice(last_weights).astype(BF16)
    four = twice(twice(0.5 * last_weights))
    w3p[...] = jnp.concatenate([four, jnp.zeros((128 - 4 * POOL_ROWS, 4 * width), F32)], axis=0).T[
        :, : 4 * POOL_ROWS
    ].astype(BF16)
    bias = jnp.concatenate([b3_ref[...], jnp.zeros((1, width - pools), F32)], axis=1)
    bias = jnp.broadcast_to(bias, (width, width)).T[:POOL_ROWS]
    b3c[...] = jnp.concatenate([bias, bias], axis=0)
    weight[...] = frac_ref[...] * mask_ref[...].astype(F32)
    owners[...] = owner_ref[...]

    for row in range(rows):
        shifted[row * taps : (row + 1) * taps, :] = three_taps(fields_ref[row].astype(F32))


def step_kernel(
    count_all,
    masks,
    pools,
    *refs,

):
    sent_ref, *got_refs = refs[: len(masks) + 1]
    shifted, weight, owner_ref, w1t, w2t, w2d, w3t, w3p, b3c = refs[len(masks) + 1 : len(masks) + 10]
    keep_ref, send_ref, coarse_ref = refs[len(masks) + 10 : len(masks) + 13]
    lower, upper, pre_one, pre_two, hidden_one, slope_one, hidden_two, slope_two = refs[
        len(masks) + 13 : len(masks) + 21
    ]
    raw_all, scale, d_raw_all, d_two_all, d_one_all, total = refs[len(masks) + 21 :]
    rows, cols = weight.shape
    channels = lower.shape[0] // 12
    width = w2d.shape[0] // 2
    tiles = rows // SIDE
    across = cols // SIDE
    blocks = tiles * across
    taps = 3 * channels
    conv_rows = 3 * taps
    cells = SIDE * cols // 2
    position = lax.axis_index("space")
    core = lax.rem(position, 2)

    outer, inner = [ref[ref.shape[0] - channels :, :] for ref in got_refs[-2:]]
    peers = owner_ref.shape[0] * 128 // blocks
    outer = jnp.where((position == 0) | (position == peers - 1), 0.0, outer)
    low = jnp.where(core == 0, outer, inner)
    high = jnp.where(core == 0, inner, outer)
    lower[:taps, :] = three_taps(low)
    lower[taps:, :] = shifted[:conv_rows, :]
    upper[:conv_rows, :] = shifted[rows * taps - conv_rows :, :]
    upper[conv_rows:, :] = three_taps(high)

    ones = jnp.ones((POOL_ROWS, cells), BF16)

    def taps_of(tile, start, count):
        parts = []
        for i in range(start, start + count):
            row = tile * SIDE + 2 * i - 1
            if row < 0:
                parts.append(lower[...])
            elif row + 4 > rows:
                parts.append(upper[...])
            else:
                parts.append(shifted[row * taps : (row + 4) * taps, :])
        return jnp.concatenate(
            [jnp.concatenate(parts, axis=1), ones[:, : count * cols]], axis=0
        )

    def wide(values, count):
        return jnp.concatenate([values] * count, axis=1)

    parts = [slice(at, at + PART) for at in range(0, cells, PART)]
    pairs = PART // cols

    def first_layer(tile, group):
        here = parts[group]
        pre_one[tile % 2, :, here] = mm(w1t[...], taps_of(tile, group * pairs, pairs))

    for group in range(len(parts)):
        first_layer(0, group)
    halves = (slice(0, width), slice(width, 2 * width))
    for tile in range(tiles):
        now = tile % 2
        for group, here in enumerate(parts):
            if tile + 1 < tiles:
                first_layer(tile + 1, group)
            for rows_of in halves:
                value, slope = gelu_pair(pre_one[now, rows_of, here])
                hidden_one[tile, rows_of, here] = value.astype(BF16)
                slope_one[tile, rows_of, here] = slope
            hidden = jnp.concatenate([hidden_one[tile, :, here], ones[:, :PART]], axis=0)
            pre_two[now, :, here] = mm(w2t[...], hidden)
        if tile > 0:
            raw_all[tile - 1] = mm(w3t[...], hidden_two[tile - 1])
        for here in parts:
            for rows_of in halves:
                value, slope = gelu_pair(pre_two[now, rows_of, here])
                hidden_two[tile, rows_of, here] = value.astype(BF16)
                slope_two[tile, rows_of, here] = slope
    raw_all[tiles - 1] = mm(w3t[...], hidden_two[tiles - 1])

    def over_rows(values):
        both = sum(values[:, i * cols : (i + 1) * cols] for i in range(SIDE // 2))
        return both[:POOL_ROWS] + both[POOL_ROWS:]

    sums = []
    for tile in range(tiles):
        raw = raw_all[tile] + wide(b3c[...], SIDE // 2)
        weights = [
            jnp.broadcast_to(weight[tile * SIDE + i : tile * SIDE + i + 1, :], (POOL_ROWS, cols))
            for i in range(SIDE)
        ]
        weights = jnp.concatenate(
            [jnp.concatenate(weights[i : i + 2], axis=0) for i in range(0, SIDE, 2)], axis=1
        )
        small = jnp.exp(-jnp.abs(raw))
        density = (jnp.maximum(raw, 0.0) + jnp.log1p(small)) * weights
        scale[tile] = jnp.where(raw >= 0.0, 1.0, small) / (1.0 + small) * weights
        sums.append(over_rows(density))
    weight_cols = jnp.sum(weight[...].reshape(tiles, SIDE, cols), axis=1)
    weight_cols = jnp.concatenate([weight_cols, jnp.zeros((-tiles % 8, cols), F32)], axis=0)
    same = ones_where(iota((cols, cols), 0) // SIDE == iota((cols, cols), 1) // SIDE)
    summed = picked(jnp.concatenate(sums + [weight_cols], axis=0), same)
    owners = owners_of(owner_ref, position, blocks)
    target = jnp.zeros((POOL_ROWS, blocks), F32)
    held = [(0, sent_ref, 0)]
    for got_ref, mask in zip(got_refs, masks):
        held = held + [(mask ^ other, got_ref, at) for at, (other, _, _) in enumerate(held)]
    for mask, ref, at in held:
        places = iota((blocks, blocks), 0) + (position ^ mask) * blocks
        packed = ref[at * PACK_ROWS : (at + 1) * PACK_ROWS, :]
        target = target + picked(unpack(packed, blocks), ones_where(places == owners))
    in_tile = iota((blocks, cols), 0) - iota((blocks, cols), 1) // SIDE
    spread = jnp.concatenate([ones_where(in_tile == tile * across) for tile in range(tiles)], axis=1)
    target_cols = picked(target, spread)
    first = iota((cols, blocks), 0)
    in_block = iota((cols, blocks), 1) - first // SIDE
    coarse = jnp.zeros((POOL_ROWS, blocks), F32)
    loss = jnp.zeros((POOL_ROWS, cols), F32)
    valid = iota((POOL_ROWS, cols), 0) < pools
    out_bias = jnp.zeros((POOL_ROWS, cols), F32)
    for tile in range(tiles):
        denom = jnp.maximum(summed[tiles * POOL_ROWS + tile : tiles * POOL_ROWS + tile + 1], 1.0)
        pred = summed[tile * POOL_ROWS : (tile + 1) * POOL_ROWS] / denom
        residual = jnp.where(valid, pred - target_cols[:, tile * cols : (tile + 1) * cols], 0.0)
        loss = loss + residual * residual
        d_cols = residual / (math.sqrt(count_all) * denom)
        d_cols = jnp.concatenate([d_cols, d_cols], axis=0)
        d_raw = (wide(d_cols, SIDE // 2) * scale[tile]).astype(BF16)
        d_raw_all[tile] = d_raw
        out_bias = out_bias + over_rows(d_raw.astype(F32))
        leads = (first % SIDE == 0) & (in_block == tile * across)
        coarse = coarse + picked(pred, ones_where(leads))
    loss = jnp.sum(jnp.sum(loss, axis=1, keepdims=True), axis=0, keepdims=True) * (1.0 / SIDE)
    coarse_rows = pack(coarse)
    coarse_ref[...] = coarse_rows

    mix_at = conv_rows
    out_at = mix_at + width
    bias_at = out_at + POOL_ROWS
    total[...] = jnp.zeros_like(total)

    def to_second(tile):
        d_raw = jnp.concatenate([d_raw_all[tile, :, here] for here in parts], axis=0)
        back = mm(w3p[...], d_raw)
        for group, here in enumerate(parts):
            d_two = back[2 * group * width : 2 * (group + 1) * width] * slope_two[tile, :, here]
            d_two_all[tile % 2, :, here] = d_two.astype(BF16)

    def to_first(tile):
        for here in parts:
            d_one = mm(w2d[...], d_two_all[tile % 2, :, here]) * slope_one[tile, :, here]
            d_one_all[tile % 2, :, here] = d_one.astype(BF16)

    def add_upper(tile):
        got = mm_nt(d_raw_all[tile], hidden_two[tile])
        total[out_at:bias_at, :] += got[:POOL_ROWS, :width] + got[POOL_ROWS:, width:]
        got = mm_nt(jnp.concatenate([hidden_one[tile], ones], axis=0), d_two_all[tile % 2])
        total[mix_at:out_at, :] += got[:width, :width] + got[width : 2 * width, width:]
        extra = got[2 * width : 2 * width + 8]
        total[bias_at + 8 : bias_at + 16, :] += extra[:, :width] + extra[:, width:]

    def add_lower(tile):
        got = mm_nt(taps_of(tile, 0, SIDE // 2), d_one_all[tile % 2])
        total[:conv_rows, :] += got[:conv_rows, :width] + got[taps : taps + conv_rows, width:]
        extra = got[taps + conv_rows : taps + conv_rows + 8]
        total[bias_at : bias_at + 8, :] += extra[:, :width] + extra[:, width:]

    to_second(0)
    to_first(0)
    for tile in range(1, tiles):
        to_second(tile)
        add_upper(tile - 1)
        to_first(tile)
        add_lower(tile - 1)
    add_upper(tiles - 1)
    add_lower(tiles - 1)

    bias = jnp.sum(out_bias, axis=1, keepdims=True)
    here, there = iota((POOL_ROWS, cols), 0), iota((POOL_ROWS, cols), 1)
    bias_row = jnp.sum(jnp.where(here == there, bias, 0.0), axis=0, keepdims=True)
    last = total[out_at:bias_at, :]
    last = jnp.where(here == pools, bias_row, last)
    total[out_at:bias_at, :] = jnp.where(here == pools + 1, loss, last)
    half = keep_ref.shape[0]
    keep_ref[...] = total[pl.ds(pl.multiple_of(core * half, 8), half), :]
    send_ref[:half, :] = total[pl.ds(pl.multiple_of((1 - core) * half, 8), half), :]
    send_ref[half:, :] = coarse_rows


def finish_kernel(
    count_all,
    mine_ref,
    other_ref,
    owner_ref,
    coarse_ref,
    conv_ref,
    conv_bias_ref,
    mix_ref,
    mix_bias_ref,
    out_ref,
    out_bias_ref,
    loss_ref,
):
    position = lax.axis_index("space")
    core = lax.rem(position, 2)
    pools, _, blocks = coarse_ref.shape
    conv_rows, width = conv_ref.shape
    out_at = conv_rows + width
    bias_at = out_at + POOL_ROWS
    half = (bias_at + POOL_ROWS) // 2
    peers = (mine_ref.shape[0] - half) // PACK_ROWS
    mine, other = mine_ref[...], other_ref[...]
    low = jnp.where(core == 0, mine[:half], other[:half])
    high = jnp.where(core == 0, other[:half], mine[:half])
    gathered = jnp.where(core == 1, mine[half:], other[half:])
    total = jnp.concatenate([low, high], axis=0)
    conv_ref[...] = total[:conv_rows]
    mix_ref[...] = total[conv_rows:out_at]
    out_ref[...] = total[out_at : out_at + pools]
    out_bias_ref[...] = total[out_at + pools : out_at + pools + 1, :pools]
    loss_ref[...] = (0.5 / count_all) * total[out_at + pools + 1 : out_at + pools + 2, :1]
    conv_bias_ref[...] = total[bias_at : bias_at + 1]
    mix_bias_ref[...] = total[bias_at + 8 : bias_at + 9]
    base = position | 1
    coarse = jnp.zeros((POOL_ROWS, blocks), F32)
    for peer in range(peers):
        owners = owners_of(owner_ref, base ^ peer, blocks)
        places = iota((blocks, blocks), 0) + position * blocks
        values = unpack(gathered[peer * PACK_ROWS : (peer + 1) * PACK_ROWS], blocks)
        got = mm_nt(thirds(values), ones_where(places == owners))
        coarse = coarse + got[:POOL_ROWS] + got[POOL_ROWS : 2 * POOL_ROWS] + got[2 * POOL_ROWS :]
    coarse_ref[:, 0, :] = coarse[:pools]


def bits_of(size, low):
    return [1 << k for k in range(size.bit_length() - 1) if (1 << k) >= low]


def swapped(values, axis, bit):
    return lax.ppermute(values, axis, [(i, i ^ bit) for i in range(lax.axis_size(axis))])


def crossed(values, step):
    dp, space = lax.axis_size("dp"), lax.axis_size("space")
    dp_moves = [(bit, 0) for bit in bits_of(dp, 1)]
    space_moves = [(0, bit) for bit in bits_of(space, 2)]
    orders = (dp_moves + space_moves, space_moves + dp_moves)
    pairs = []
    for d in range(dp):
        for s in range(space):
            d_bit, s_bit = orders[s % 2][step]
            pairs.append((d * space + s, (d ^ d_bit) * space + (s ^ s_bit)))
    return lax.ppermute(values, ("dp", "space"), pairs)


def reduce_all(keep, send, coarse):
    space = lax.axis_size("space")
    n_dp, n_space = len(bits_of(lax.axis_size("dp"), 1)), len(bits_of(space, 2))
    rows = keep.shape[0]
    got = swapped(send, "space", 1)
    half = keep + got[:rows]
    gathered = jnp.concatenate([coarse, got[rows:]], axis=0)
    for step in range(n_dp + n_space):
        if step < n_space:
            got = crossed(jnp.concatenate([half, gathered], axis=0), step)
            gathered = jnp.concatenate([gathered, got[rows:]], axis=0)
            got = got[:rows]
        else:
            got = crossed(half, step)
        half = half + got
    mine = jnp.concatenate([half, gathered], axis=0)
    return mine, swapped(mine, "space", 1)


def on_device(
    fields,
    land_mask,
    land_frac,
    owner_map,
    targets,
    conv_weight,
    conv_bias,
    mix_weight,
    mix_bias,
    out_weight,
    out_bias,
):
    peers = lax.axis_size("space")
    pools = out_weight.shape[1]
    width = mix_weight.shape[0]
    channels, rows, cols = fields.shape[1:]
    tiles = rows // SIDE
    blocks = tiles * (cols // SIDE)
    count_all = lax.axis_size("dp") * pools * owner_map.shape[0]
    owners = owner_map.reshape(-1, 128)
    position = lax.axis_index("space")
    masks = bits_of(peers, 4)[::-1] + [3, 1]
    apart = jnp.where(position % 2 == 0, position ^ (position - 1), position ^ (position + 1))
    sent, outer, inner = pl.pallas_call(
        pack_kernel,
        out_shape=[
            pltpu.VMEM((PACK_ROWS + channels, cols), F32),
            pltpu.VMEM((channels, cols), F32),
            pltpu.VMEM((channels, cols), F32),
        ],
        in_specs=[pl.BlockSpec(memory_space=pltpu.HBM)] * 2,
        out_specs=[pl.BlockSpec(memory_space=pltpu.VMEM)] * 3,
        compiler_params=pltpu.CompilerParams(vmem_limit_bytes=ALL_VMEM),
        scratch_shapes=[
            pltpu.VMEM((channels, 16, cols), BF16),
            pltpu.VMEM((channels, 16, cols), BF16),
            pltpu.VMEM((pools, 1, blocks), F32),
            pltpu.SemaphoreType.DMA((3,)),
        ],
        name="pack_edges",
    )(fields, jnp.swapaxes(targets, 0, 1))
    payload, gots = sent, []
    for at, mask in enumerate(masks):
        if mask == 1:
            payload = jnp.concatenate([held, inner], axis=0)
        elif at > 0:
            mine = apart == (mask if mask == 3 else 2 * mask - 1)
            payload = jnp.concatenate([held, jnp.where(mine, outer, passing)], axis=0)
        got = swapped(payload, "space", mask)
        gots.append(got)
        had = payload.shape[0] - channels
        held = jnp.concatenate([payload[:had], got[:had]], axis=0)
        passing = got[had:]
    later, _ = lax.optimization_barrier((fields, sent))
    by_row = jnp.swapaxes(later[0], 0, 1)
    by_row, _ = lax.optimization_barrier((by_row, gots[0]))

    conv_rows = 9 * channels
    half = conv_rows + width + 2 * POOL_ROWS
    half = (half + 31) // 32 * 16
    cells = SIDE * cols // 2
    f32, bf16 = F32, BF16
    prepared = pl.pallas_call(
        prepare_kernel,
        out_shape=[
            pltpu.VMEM((rows * 3 * channels, cols), bf16),
            pltpu.VMEM((rows, cols), f32),
            pltpu.VMEM(owners.shape, jnp.int32),
            pltpu.VMEM((2 * width, conv_rows + 3 * channels + POOL_ROWS), bf16),
            pltpu.VMEM((2 * width, 2 * width + POOL_ROWS), bf16),
            pltpu.VMEM((2 * width, 2 * width), bf16),
            pltpu.VMEM((2 * POOL_ROWS, 2 * width), bf16),
            pltpu.VMEM((4 * width, 4 * POOL_ROWS), bf16),
            pltpu.VMEM((2 * POOL_ROWS, cols), f32),
        ],
        in_specs=[pl.BlockSpec(memory_space=pltpu.VMEM)] * 10,
        out_specs=[pl.BlockSpec(memory_space=pltpu.VMEM)] * 9,
        compiler_params=pltpu.CompilerParams(vmem_limit_bytes=PREPARE_VMEM),
        cost_estimate=pl.CostEstimate(flops=10**9, bytes_accessed=4 * 10**6, transcendentals=0),
        name="prepare",
    )(
        by_row,
        land_frac,
        land_mask,
        conv_weight.reshape(conv_rows, width),
        conv_bias.reshape(1, width),
        mix_weight,
        mix_bias.reshape(1, width),
        out_weight.T,
        out_bias.reshape(1, pools),
        owners,
    )
    owners = prepared[2]
    keep, send, coarse = pl.pallas_call(
        functools.partial(step_kernel, count_all, masks, pools),
        out_shape=[
            jax.ShapeDtypeStruct((half, width), f32),
            jax.ShapeDtypeStruct((half + PACK_ROWS, width), f32),
            jax.ShapeDtypeStruct((PACK_ROWS, width), f32),
        ],
        in_specs=[pl.BlockSpec(memory_space=pltpu.VMEM)] * (len(masks) + 10),
        out_specs=[pl.BlockSpec(memory_space=pltpu.VMEM)] * 3,
        scratch_shapes=[
            pltpu.VMEM((12 * channels, cols), bf16),
            pltpu.VMEM((12 * channels, cols), bf16),
            pltpu.VMEM((2, 2 * width, cells), f32),
            pltpu.VMEM((2, 2 * width, cells), f32),
            pltpu.VMEM((tiles, 2 * width, cells), bf16),
            pltpu.VMEM((tiles, 2 * width, cells), f32),
            pltpu.VMEM((tiles, 2 * width, cells), bf16),
            pltpu.VMEM((tiles, 2 * width, cells), f32),
            pltpu.VMEM((tiles, 2 * POOL_ROWS, cells), f32),
            pltpu.VMEM((tiles, 2 * POOL_ROWS, cells), f32),
            pltpu.VMEM((tiles, 2 * POOL_ROWS, cells), bf16),
            pltpu.VMEM((2, 2 * width, cells), bf16),
            pltpu.VMEM((2, 2 * width, cells), bf16),
            pltpu.VMEM((2 * half, width), f32),
        ],
        compiler_params=pltpu.CompilerParams(vmem_limit_bytes=VMEM),
        name="train_step",
    )(
        sent,
        *gots,
        *prepared,
    )
    mine, other = reduce_all(keep, send, coarse)
    outs = pl.pallas_call(
        functools.partial(finish_kernel, count_all),
        out_shape=[
            jax.ShapeDtypeStruct((pools, 1, blocks), f32),
            jax.ShapeDtypeStruct((conv_rows, width), f32),
            jax.ShapeDtypeStruct((1, width), f32),
            jax.ShapeDtypeStruct((width, width), f32),
            jax.ShapeDtypeStruct((1, width), f32),
            jax.ShapeDtypeStruct((pools, width), f32),
            jax.ShapeDtypeStruct((1, pools), f32),
            jax.ShapeDtypeStruct((1, 1), f32),
        ],
        in_specs=[pl.BlockSpec(memory_space=pltpu.VMEM)] * 3,
        out_specs=[pl.BlockSpec(memory_space=pltpu.VMEM)] * 8,
        compiler_params=pltpu.CompilerParams(vmem_limit_bytes=VMEM),
        name="finish",
    )(mine, other, owners)
    coarse_pred, conv_grad, conv_bias_grad, mix_grad, mix_bias_grad, out_grad, out_bias_grad, loss = outs
    return (
        jnp.swapaxes(coarse_pred, 0, 1),
        conv_grad.reshape(conv_weight.shape),
        conv_bias_grad.reshape(width),
        mix_grad,
        mix_bias_grad.reshape(width),
        out_grad.T,
        out_bias_grad.reshape(pools),
        loss.reshape(()),
    )


def solution(mesh):
    placed = (
        P("dp", None, "space", None),
        P("space", None),
        P("space", None),
        P(),
        P("dp", None, "space"),
        P(),
        P(),
        P(),
        P(),
        P(),
        P(),
    )
    return jax.shard_map(
        on_device,
        mesh=mesh,
        in_specs=placed,
        out_specs=(P("dp", None, "space"), P(), P(), P(), P(), P(), P(), P()),
        check_vma=False,
    )
```

```python
import functools
import math

import jax
import jax.numpy as jnp
from jax import lax
from jax.experimental import pallas as pl
from jax.experimental.pallas import tpu as pltpu
from jax.sharding import PartitionSpec as P

SIDE = 8
POOL_ROWS = 16
PACK_ROWS = 24
MOST_PICKS = 8
PART = 256
VMEM = 46 * 1024 * 1024
PREPARE_VMEM = 8 * 1024 * 1024
ALL_VMEM = 127 * 512 * 1024

CUBIC = 0.044715
ROOT_TWO_PI = math.sqrt(2.0 / math.pi)

F32, BF16 = jnp.float32, jnp.bfloat16


def gelu_pair(half):
    square = half * half
    tanh_value = jnp.tanh(half * (2.0 * ROOT_TWO_PI + (8.0 * ROOT_TWO_PI * CUBIC) * square))
    above = 1.0 + tanh_value
    value = half * above
    slope = above + value * (1.0 - tanh_value) * (2.0 * ROOT_TWO_PI + (24.0 * ROOT_TWO_PI * CUBIC) * square)
    return value, slope


def mm(left, right):
    return jnp.dot(left, right, preferred_element_type=F32)


def mm_nt(left, right):
    return lax.dot_general(left, right, (((1,), (1,)), ((), ())), preferred_element_type=F32)


def thirds(values):
    high = values.astype(BF16)
    rest = values - high.astype(F32)
    middle = rest.astype(BF16)
    low = (rest - middle.astype(F32)).astype(BF16)
    return jnp.concatenate([high, middle, low], axis=0)


def picked(values, chosen):
    rows = values.shape[0]
    out = mm(thirds(values), chosen)
    return out[:rows] + out[rows : 2 * rows] + out[2 * rows :]


def ones_where(condition):
    return jnp.where(condition, 1.0, 0.0).astype(BF16)


def iota(shape, dim):
    return lax.broadcasted_iota(jnp.int32, shape, dim)


def pack(values):
    tails = jnp.concatenate([values[:8, 128:], values[8:, 128:]], axis=1)
    return jnp.concatenate([values[:, :128], tails], axis=0)


def unpack(packed, blocks):
    tails = packed[POOL_ROWS:]
    tails = jnp.concatenate([tails[:, : blocks - 128], tails[:, blocks - 128 :]], axis=0)
    return jnp.concatenate([packed[:POOL_ROWS], tails], axis=1)


def owners_of(owner_ref, strip, blocks):
    at = strip * blocks
    row = at // 128
    pair = jnp.concatenate([owner_ref[pl.ds(row, 1), :], owner_ref[pl.ds(row + 1, 1), :]], axis=1)
    return jnp.where(at % 128 == 0, pair, pltpu.roll(pair, 256 - blocks % 128, 1))[:, :blocks]


def three_taps(row):
    lane = iota(row.shape, 1)
    last = row.shape[1] - 1
    left = jnp.where(lane == 0, 0.0, pltpu.roll(row, 1, 1))
    right = jnp.where(lane == last, 0.0, pltpu.roll(row, last, 1))
    return jnp.concatenate([left, row, right], axis=0).astype(BF16)


def pack_kernel(
    fields_ref, target_ref, sent_ref, outer_ref, inner_ref, top_rows, bottom_rows, targets, done
):
    rows, some = fields_ref.shape[2], top_rows.shape[1]
    copies = [
        pltpu.make_async_copy(fields_ref.at[0, :, pl.ds(0, some), :], top_rows, done.at[0]),
        pltpu.make_async_copy(fields_ref.at[0, :, pl.ds(rows - some, some), :], bottom_rows, done.at[1]),
        pltpu.make_async_copy(target_ref, targets, done.at[2]),
    ]
    for copy in copies:
        copy.start()
    for copy in copies:
        copy.wait()
    core = lax.rem(lax.axis_index("space"), 2)
    pools, _, blocks = target_ref.shape
    top = top_rows[...].astype(F32)[:, 0, :]
    bottom = bottom_rows[...].astype(F32)[:, some - 1, :]
    values = jnp.concatenate(
        [targets[:, 0, :], jnp.zeros((POOL_ROWS - pools, blocks), F32)], axis=0
    )
    sent_ref[:PACK_ROWS, :] = pack(values)
    sent_ref[PACK_ROWS:, :] = jnp.where(core == 0, top, bottom)
    outer_ref[...] = jnp.where(core == 0, top, bottom)
    inner_ref[...] = jnp.where(core == 0, bottom, top)


def picks_of(mine, owner):
    blocks = mine.shape[1]
    return ones_where(iota((blocks, blocks), 0) == mine - owner * blocks)


def prepare_kernel(
    held,
    fields_ref,
    frac_ref,
    mask_ref,
    w1_ref,
    b1_ref,
    w2_ref,
    b2_ref,
    w3t_ref,
    b3_ref,
    owner_ref,
    shifted,
    weight,
    owners,
    w1t,
    w2t,
    w2d,
    w3t,
    w3p,
    b3c,
    picks,
    spread,
    leads,
):
    rows, channels, cols = fields_ref.shape
    width = w2_ref.shape[0]
    pools = w3t_ref.shape[0]
    taps = 3 * channels

    def terms(bias):
        high = bias.astype(BF16).astype(F32)
        middle = (bias - high).astype(BF16).astype(F32)
        fill = jnp.zeros((POOL_ROWS - 3, bias.shape[1]), F32)
        return jnp.concatenate([high, middle, bias - high - middle, fill], axis=0)

    def twice(values):
        none = jnp.zeros_like(values)
        return jnp.concatenate(
            [jnp.concatenate([values, none], axis=1), jnp.concatenate([none, values], axis=1)], axis=0
        )

    def doubled(values):
        return jnp.concatenate([values, values], axis=1)

    first_weights, none = 0.5 * w1_ref[...].astype(F32), jnp.zeros((taps, width), F32)
    bias = terms(0.5 * b1_ref[...])
    w1t[:width, :] = jnp.concatenate([first_weights, none, bias], axis=0).T.astype(BF16)
    w1t[width:, :] = jnp.concatenate([none, first_weights, bias], axis=0).T.astype(BF16)
    second_weights = twice(0.5 * w2_ref[...].astype(F32))
    w2d[...] = second_weights.astype(BF16)
    w2t[...] = jnp.concatenate([second_weights, doubled(terms(0.5 * b2_ref[...]))], axis=0).T.astype(BF16)
    last_weights = jnp.concatenate(
        [w3t_ref[...].astype(F32), jnp.zeros((POOL_ROWS - pools, width), F32)], axis=0
    )
    w3t[...] = twice(last_weights).astype(BF16)
    four = twice(twice(0.5 * last_weights))
    w3p[...] = jnp.concatenate([four, jnp.zeros((128 - 4 * POOL_ROWS, 4 * width), F32)], axis=0).T[
        :, : 4 * POOL_ROWS
    ].astype(BF16)
    bias = jnp.concatenate([b3_ref[...], jnp.zeros((1, width - pools), F32)], axis=1)
    bias = jnp.broadcast_to(bias, (width, width)).T[:POOL_ROWS]
    b3c[...] = jnp.concatenate([bias, bias], axis=0)
    weight[...] = frac_ref[...] * mask_ref[...].astype(F32)
    owners[...] = owner_ref[...]

    position = lax.axis_index("space")
    blocks = picks.shape[1]
    mine = owners_of(owner_ref, position, blocks)
    for at, mask in enumerate(held[: picks.shape[0] // blocks]):
        picks[at * blocks : (at + 1) * blocks, :] = picks_of(mine, position ^ mask)
    tiles, across = rows // SIDE, cols // SIDE
    in_tile = iota((blocks, cols), 0) - iota((blocks, cols), 1) // SIDE
    first = iota((cols, blocks), 0)
    in_block = jnp.where(first % SIDE == 0, iota((cols, blocks), 1) - first // SIDE, -1)
    for tile in range(tiles):
        spread[:, tile * cols : (tile + 1) * cols] = ones_where(in_tile == tile * across)
        leads[tile * cols : (tile + 1) * cols, :] = ones_where(in_block == tile * across)

    for row in range(rows):
        shifted[row * taps : (row + 1) * taps, :] = three_taps(fields_ref[row].astype(F32))


def step_kernel(
    count_all,
    masks,
    pools,
    *refs,

):
    sent_ref, *got_refs = refs[: len(masks) + 1]
    shifted, weight, owner_ref, w1t, w2t, w2d, w3t, w3p, b3c, picks, spread, leads = refs[
        len(masks) + 1 : len(masks) + 13
    ]
    keep_ref, send_ref, coarse_ref = refs[len(masks) + 13 : len(masks) + 16]
    lower, upper, pre_one, pre_two, hidden_one, slope_one, hidden_two, slope_two = refs[
        len(masks) + 16 : len(masks) + 24
    ]
    raw_all, scale, d_raw_all, d_two_all, d_one_all, total = refs[len(masks) + 24 :]
    rows, cols = weight.shape
    channels = lower.shape[0] // 12
    width = w2d.shape[0] // 2
    tiles = rows // SIDE
    across = cols // SIDE
    blocks = tiles * across
    taps = 3 * channels
    conv_rows = 3 * taps
    cells = SIDE * cols // 2
    position = lax.axis_index("space")
    core = lax.rem(position, 2)

    outer, inner = [ref[ref.shape[0] - channels :, :] for ref in got_refs[-2:]]
    peers = owner_ref.shape[0] * 128 // blocks
    outer = jnp.where((position == 0) | (position == peers - 1), 0.0, outer)
    low = jnp.where(core == 0, outer, inner)
    high = jnp.where(core == 0, inner, outer)
    lower[:taps, :] = three_taps(low)
    lower[taps:, :] = shifted[:conv_rows, :]
    upper[:conv_rows, :] = shifted[rows * taps - conv_rows :, :]
    upper[conv_rows:, :] = three_taps(high)

    ones = jnp.ones((POOL_ROWS, cells), BF16)

    def taps_of(tile, start, count):
        parts = []
        for i in range(start, start + count):
            row = tile * SIDE + 2 * i - 1
            if row < 0:
                parts.append(lower[...])
            elif row + 4 > rows:
                parts.append(upper[...])
            else:
                parts.append(shifted[row * taps : (row + 4) * taps, :])
        return jnp.concatenate(
            [jnp.concatenate(parts, axis=1), ones[:, : count * cols]], axis=0
        )

    def wide(values, count):
        return jnp.concatenate([values] * count, axis=1)

    parts = [slice(at, at + PART) for at in range(0, cells, PART)]
    pairs = PART // cols

    def first_layer(tile, group):
        here = parts[group]
        pre_one[tile % 2, :, here] = mm(w1t[...], taps_of(tile, group * pairs, pairs))

    for group in range(len(parts)):
        first_layer(0, group)
    halves = (slice(0, width), slice(width, 2 * width))
    for tile in range(tiles):
        now = tile % 2
        for group, here in enumerate(parts):
            if tile + 1 < tiles:
                first_layer(tile + 1, group)
            for rows_of in halves:
                value, slope = gelu_pair(pre_one[now, rows_of, here])
                hidden_one[tile, rows_of, here] = value.astype(BF16)
                slope_one[tile, rows_of, here] = slope
            hidden = jnp.concatenate([hidden_one[tile, :, here], ones[:, :PART]], axis=0)
            pre_two[now, :, here] = mm(w2t[...], hidden)
        if tile > 0:
            raw_all[tile - 1] = mm(w3t[...], hidden_two[tile - 1])
        for here in parts:
            for rows_of in halves:
                value, slope = gelu_pair(pre_two[now, rows_of, here])
                hidden_two[tile, rows_of, here] = value.astype(BF16)
                slope_two[tile, rows_of, here] = slope
    raw_all[tiles - 1] = mm(w3t[...], hidden_two[tiles - 1])

    def over_rows(values):
        both = sum(values[:, i * cols : (i + 1) * cols] for i in range(SIDE // 2))
        return both[:POOL_ROWS] + both[POOL_ROWS:]

    sums = []
    for tile in range(tiles):
        raw = raw_all[tile] + wide(b3c[...], SIDE // 2)
        weights = [
            jnp.broadcast_to(weight[tile * SIDE + i : tile * SIDE + i + 1, :], (POOL_ROWS, cols))
            for i in range(SIDE)
        ]
        weights = jnp.concatenate(
            [jnp.concatenate(weights[i : i + 2], axis=0) for i in range(0, SIDE, 2)], axis=1
        )
        small = jnp.exp(-jnp.abs(raw))
        density = (jnp.maximum(raw, 0.0) + jnp.log1p(small)) * weights
        scale[tile] = jnp.where(raw >= 0.0, 1.0, small) / (1.0 + small) * weights
        sums.append(over_rows(density))
    weight_cols = jnp.sum(weight[...].reshape(tiles, SIDE, cols), axis=1)
    weight_cols = jnp.concatenate([weight_cols, jnp.zeros((-tiles % 8, cols), F32)], axis=0)
    same = ones_where(iota((cols, cols), 0) // SIDE == iota((cols, cols), 1) // SIDE)
    summed = picked(jnp.concatenate(sums + [weight_cols], axis=0), same)
    target = jnp.zeros((POOL_ROWS, blocks), F32)
    held = [(0, sent_ref, 0)]
    for got_ref, mask in zip(got_refs, masks):
        held = held + [(mask ^ other, got_ref, at) for at, (other, _, _) in enumerate(held)]
    mine = owners_of(owner_ref, position, blocks)
    for number, (mask, ref, at) in enumerate(held):
        packed = ref[at * PACK_ROWS : (at + 1) * PACK_ROWS, :]
        if (number + 1) * blocks <= picks.shape[0]:
            chosen = picks[number * blocks : (number + 1) * blocks, :]
        else:
            chosen = picks_of(mine, position ^ mask)
        target = target + picked(unpack(packed, blocks), chosen)
    target_cols = picked(target, spread[...])
    coarse = jnp.zeros((POOL_ROWS, blocks), F32)
    loss = jnp.zeros((POOL_ROWS, cols), F32)
    valid = iota((POOL_ROWS, cols), 0) < pools
    out_bias = jnp.zeros((POOL_ROWS, cols), F32)
    for tile in range(tiles):
        denom = jnp.maximum(summed[tiles * POOL_ROWS + tile : tiles * POOL_ROWS + tile + 1], 1.0)
        pred = summed[tile * POOL_ROWS : (tile + 1) * POOL_ROWS] / denom
        residual = jnp.where(valid, pred - target_cols[:, tile * cols : (tile + 1) * cols], 0.0)
        loss = loss + residual * residual
        d_cols = residual / (math.sqrt(count_all) * denom)
        d_cols = jnp.concatenate([d_cols, d_cols], axis=0)
        d_raw = (wide(d_cols, SIDE // 2) * scale[tile]).astype(BF16)
        d_raw_all[tile] = d_raw
        out_bias = out_bias + over_rows(d_raw.astype(F32))
        coarse = coarse + picked(pred, leads[tile * cols : (tile + 1) * cols, :])
    loss = jnp.sum(jnp.sum(loss, axis=1, keepdims=True), axis=0, keepdims=True) * (1.0 / SIDE)
    coarse_rows = pack(coarse)
    coarse_ref[...] = coarse_rows

    mix_at = conv_rows
    out_at = mix_at + width
    bias_at = out_at + POOL_ROWS
    total[...] = jnp.zeros_like(total)

    def to_second(tile):
        d_raw = jnp.concatenate([d_raw_all[tile, :, here] for here in parts], axis=0)
        back = mm(w3p[...], d_raw)
        for group, here in enumerate(parts):
            d_two = back[2 * group * width : 2 * (group + 1) * width] * slope_two[tile, :, here]
            d_two_all[tile % 2, :, here] = d_two.astype(BF16)

    def to_first(tile):
        for here in parts:
            d_one = mm(w2d[...], d_two_all[tile % 2, :, here]) * slope_one[tile, :, here]
            d_one_all[tile % 2, :, here] = d_one.astype(BF16)

    def add_upper(tile):
        got = mm_nt(d_raw_all[tile], hidden_two[tile])
        total[out_at:bias_at, :] += got[:POOL_ROWS, :width] + got[POOL_ROWS:, width:]
        got = mm_nt(jnp.concatenate([hidden_one[tile], ones], axis=0), d_two_all[tile % 2])
        total[mix_at:out_at, :] += got[:width, :width] + got[width : 2 * width, width:]
        extra = got[2 * width : 2 * width + 8]
        total[bias_at + 8 : bias_at + 16, :] += extra[:, :width] + extra[:, width:]

    def add_lower(tile):
        got = mm_nt(taps_of(tile, 0, SIDE // 2), d_one_all[tile % 2])
        total[:conv_rows, :] += got[:conv_rows, :width] + got[taps : taps + conv_rows, width:]
        extra = got[taps + conv_rows : taps + conv_rows + 8]
        total[bias_at : bias_at + 8, :] += extra[:, :width] + extra[:, width:]

    to_second(0)
    to_first(0)
    for tile in range(1, tiles):
        to_second(tile)
        add_upper(tile - 1)
        to_first(tile)
        add_lower(tile - 1)
    add_upper(tiles - 1)
    add_lower(tiles - 1)

    bias = jnp.sum(out_bias, axis=1, keepdims=True)
    here, there = iota((POOL_ROWS, cols), 0), iota((POOL_ROWS, cols), 1)
    bias_row = jnp.sum(jnp.where(here == there, bias, 0.0), axis=0, keepdims=True)
    last = total[out_at:bias_at, :]
    last = jnp.where(here == pools, bias_row, last)
    total[out_at:bias_at, :] = jnp.where(here == pools + 1, loss, last)
    half = keep_ref.shape[0]
    keep_ref[...] = total[pl.ds(pl.multiple_of(core * half, 8), half), :]
    send_ref[:half, :] = total[pl.ds(pl.multiple_of((1 - core) * half, 8), half), :]
    send_ref[half:, :] = coarse_rows


def finish_kernel(
    count_all,
    strides,
    mine_ref,
    other_ref,
    owner_ref,
    coarse_ref,
    conv_ref,
    conv_bias_ref,
    mix_ref,
    mix_bias_ref,
    out_ref,
    out_bias_ref,
    loss_ref,
):
    position = lax.axis_index("space")
    core = lax.rem(position, 2)
    pools, _, blocks = coarse_ref.shape
    conv_rows, width = conv_ref.shape
    out_at = conv_rows + width
    bias_at = out_at + POOL_ROWS
    half = (bias_at + POOL_ROWS) // 2
    peers = (mine_ref.shape[0] - half) // PACK_ROWS
    mine, other = mine_ref[...], other_ref[...]
    low = jnp.where(core == 0, mine[:half], other[:half])
    high = jnp.where(core == 0, other[:half], mine[:half])
    gathered = jnp.where(core == 1, mine[half:], other[half:])
    total = jnp.concatenate([low, high], axis=0)
    conv_ref[...] = total[:conv_rows]
    mix_ref[...] = total[conv_rows:out_at]
    out_ref[...] = total[out_at : out_at + pools]
    out_bias_ref[...] = total[out_at + pools : out_at + pools + 1, :pools]
    loss_ref[...] = (0.5 / count_all) * total[out_at + pools + 1 : out_at + pools + 2, :1]
    conv_bias_ref[...] = total[bias_at : bias_at + 1]
    mix_bias_ref[...] = total[bias_at + 8 : bias_at + 9]
    base = position | 1
    apart = [0]
    for bit in strides:
        apart = apart + [bit ^ other for other in apart]
    coarse = jnp.zeros((POOL_ROWS, blocks), F32)
    for peer in range(peers):
        owners = owners_of(owner_ref, base ^ apart[peer], blocks)
        places = iota((blocks, blocks), 0) + position * blocks
        values = unpack(gathered[peer * PACK_ROWS : (peer + 1) * PACK_ROWS], blocks)
        got = mm_nt(thirds(values), ones_where(places == owners))
        coarse = coarse + got[:POOL_ROWS] + got[POOL_ROWS : 2 * POOL_ROWS] + got[2 * POOL_ROWS :]
    coarse_ref[:, 0, :] = coarse[:pools]


def bits_of(size, low):
    return [1 << k for k in range(size.bit_length() - 1) if (1 << k) >= low]


def swapped(values, axis, bit):
    return lax.ppermute(values, axis, [(i, i ^ bit) for i in range(lax.axis_size(axis))])


def crossed(values, step):
    dp, space = lax.axis_size("dp"), lax.axis_size("space")
    dp_moves = [(bit, 0) for bit in bits_of(dp, 1)]
    space_moves = [(0, bit) for bit in bits_of(space, 2)[::-1]]
    orders = (dp_moves + space_moves, space_moves + dp_moves)
    pairs = []
    for d in range(dp):
        for s in range(space):
            d_bit, s_bit = orders[s % 2][step]
            pairs.append((d * space + s, (d ^ d_bit) * space + (s ^ s_bit)))
    return lax.ppermute(values, ("dp", "space"), pairs)


def reduce_all(keep, send, coarse):
    space = lax.axis_size("space")
    n_dp, n_space = len(bits_of(lax.axis_size("dp"), 1)), len(bits_of(space, 2))
    rows = keep.shape[0]
    got = swapped(send, "space", 1)
    half = keep + got[:rows]
    gathered = jnp.concatenate([coarse, got[rows:]], axis=0)
    for step in range(n_dp + n_space):
        if step < n_space:
            got = crossed(jnp.concatenate([half, gathered], axis=0), step)
            gathered = jnp.concatenate([gathered, got[rows:]], axis=0)
            got = got[:rows]
        else:
            got = crossed(half, step)
        half = half + got
    mine = jnp.concatenate([half, gathered], axis=0)
    return mine, swapped(mine, "space", 1)


def on_device(
    fields,
    land_mask,
    land_frac,
    owner_map,
    targets,
    conv_weight,
    conv_bias,
    mix_weight,
    mix_bias,
    out_weight,
    out_bias,
):
    peers = lax.axis_size("space")
    pools = out_weight.shape[1]
    width = mix_weight.shape[0]
    channels, rows, cols = fields.shape[1:]
    tiles = rows // SIDE
    blocks = tiles * (cols // SIDE)
    count_all = lax.axis_size("dp") * pools * owner_map.shape[0]
    owners = owner_map.reshape(-1, 128)
    position = lax.axis_index("space")
    masks = bits_of(peers, 4)[::-1] + [3, 1]
    apart = jnp.where(position % 2 == 0, position ^ (position - 1), position ^ (position + 1))
    sent, outer, inner = pl.pallas_call(
        pack_kernel,
        out_shape=[
            pltpu.VMEM((PACK_ROWS + channels, cols), F32),
            pltpu.VMEM((channels, cols), F32),
            pltpu.VMEM((channels, cols), F32),
        ],
        in_specs=[pl.BlockSpec(memory_space=pltpu.HBM)] * 2,
        out_specs=[pl.BlockSpec(memory_space=pltpu.VMEM)] * 3,
        compiler_params=pltpu.CompilerParams(vmem_limit_bytes=ALL_VMEM),
        scratch_shapes=[
            pltpu.VMEM((channels, 16, cols), BF16),
            pltpu.VMEM((channels, 16, cols), BF16),
            pltpu.VMEM((pools, 1, blocks), F32),
            pltpu.SemaphoreType.DMA((3,)),
        ],
        name="pack_edges",
    )(fields, jnp.swapaxes(targets, 0, 1))
    later, _ = lax.optimization_barrier((fields, sent))
    by_row = jnp.swapaxes(later[0], 0, 1)
    got = swapped(sent, "space", masks[0])
    by_row, got = lax.optimization_barrier((by_row, got))

    conv_rows = 9 * channels
    half = conv_rows + width + 2 * POOL_ROWS
    half = (half + 31) // 32 * 16
    cells = SIDE * cols // 2
    f32, bf16 = F32, BF16
    held_masks = [0]
    for mask in masks:
        held_masks = held_masks + [mask ^ other for other in held_masks]
    prepared = pl.pallas_call(
        functools.partial(prepare_kernel, held_masks),
        out_shape=[
            pltpu.VMEM((rows * 3 * channels, cols), bf16),
            pltpu.VMEM((rows, cols), f32),
            pltpu.VMEM(owners.shape, jnp.int32),
            pltpu.VMEM((2 * width, conv_rows + 3 * channels + POOL_ROWS), bf16),
            pltpu.VMEM((2 * width, 2 * width + POOL_ROWS), bf16),
            pltpu.VMEM((2 * width, 2 * width), bf16),
            pltpu.VMEM((2 * POOL_ROWS, 2 * width), bf16),
            pltpu.VMEM((4 * width, 4 * POOL_ROWS), bf16),
            pltpu.VMEM((2 * POOL_ROWS, cols), f32),
            pltpu.VMEM((min(peers, MOST_PICKS) * blocks, blocks), bf16),
            pltpu.VMEM((blocks, tiles * cols), bf16),
            pltpu.VMEM((tiles * cols, blocks), bf16),
        ],
        in_specs=[pl.BlockSpec(memory_space=pltpu.VMEM)] * 10,
        out_specs=[pl.BlockSpec(memory_space=pltpu.VMEM)] * 12,
        compiler_params=pltpu.CompilerParams(vmem_limit_bytes=PREPARE_VMEM),
        cost_estimate=pl.CostEstimate(flops=10**9, bytes_accessed=4 * 10**6, transcendentals=0),
        name="prepare",
    )(
        by_row,
        land_frac,
        land_mask,
        conv_weight.reshape(conv_rows, width),
        conv_bias.reshape(1, width),
        mix_weight,
        mix_bias.reshape(1, width),
        out_weight.T,
        out_bias.reshape(1, pools),
        owners,
    )
    payload, gots = sent, []
    for at, mask in enumerate(masks):
        if mask == 1:
            payload = jnp.concatenate([held, inner], axis=0)
        elif at > 0:
            mine = apart == (mask if mask == 3 else 2 * mask - 1)
            payload = jnp.concatenate([held, jnp.where(mine, outer, passing)], axis=0)
        if at > 0:
            got = swapped(payload, "space", mask)
        if at == 1:
            prepared, got = lax.optimization_barrier((prepared, got))
        gots.append(got)
        had = payload.shape[0] - channels
        held = jnp.concatenate([payload[:had], got[:had]], axis=0)
        passing = got[had:]
    owners = prepared[2]
    keep, send, coarse = pl.pallas_call(
        functools.partial(step_kernel, count_all, masks, pools),
        out_shape=[
            jax.ShapeDtypeStruct((half, width), f32),
            jax.ShapeDtypeStruct((half + PACK_ROWS, width), f32),
            jax.ShapeDtypeStruct((PACK_ROWS, width), f32),
        ],
        in_specs=[pl.BlockSpec(memory_space=pltpu.VMEM)] * (len(masks) + 13),
        out_specs=[pl.BlockSpec(memory_space=pltpu.VMEM)] * 3,
        scratch_shapes=[
            pltpu.VMEM((12 * channels, cols), bf16),
            pltpu.VMEM((12 * channels, cols), bf16),
            pltpu.VMEM((2, 2 * width, cells), f32),
            pltpu.VMEM((2, 2 * width, cells), f32),
            pltpu.VMEM((tiles, 2 * width, cells), bf16),
            pltpu.VMEM((tiles, 2 * width, cells), f32),
            pltpu.VMEM((tiles, 2 * width, cells), bf16),
            pltpu.VMEM((tiles, 2 * width, cells), f32),
            pltpu.VMEM((tiles, 2 * POOL_ROWS, cells), f32),
            pltpu.VMEM((tiles, 2 * POOL_ROWS, cells), f32),
            pltpu.VMEM((tiles, 2 * POOL_ROWS, cells), bf16),
            pltpu.VMEM((2, 2 * width, cells), bf16),
            pltpu.VMEM((2, 2 * width, cells), bf16),
            pltpu.VMEM((2 * half, width), f32),
        ],
        compiler_params=pltpu.CompilerParams(vmem_limit_bytes=VMEM),
        name="train_step",
    )(
        sent,
        *gots,
        *prepared,
    )
    mine, other = reduce_all(keep, send, coarse)
    outs = pl.pallas_call(
        functools.partial(finish_kernel, count_all, [1] + bits_of(peers, 2)[::-1]),
        out_shape=[
            jax.ShapeDtypeStruct((pools, 1, blocks), f32),
            jax.ShapeDtypeStruct((conv_rows, width), f32),
            jax.ShapeDtypeStruct((1, width), f32),
            jax.ShapeDtypeStruct((width, width), f32),
            jax.ShapeDtypeStruct((1, width), f32),
            jax.ShapeDtypeStruct((pools, width), f32),
            jax.ShapeDtypeStruct((1, pools), f32),
            jax.ShapeDtypeStruct((1, 1), f32),
        ],
        in_specs=[pl.BlockSpec(memory_space=pltpu.VMEM)] * 3,
        out_specs=[pl.BlockSpec(memory_space=pltpu.VMEM)] * 8,
        compiler_params=pltpu.CompilerParams(vmem_limit_bytes=VMEM),
        name="finish",
    )(mine, other, owners)
    coarse_pred, conv_grad, conv_bias_grad, mix_grad, mix_bias_grad, out_grad, out_bias_grad, loss = outs
    return (
        jnp.swapaxes(coarse_pred, 0, 1),
        conv_grad.reshape(conv_weight.shape),
        conv_bias_grad.reshape(width),
        mix_grad,
        mix_bias_grad.reshape(width),
        out_grad.T,
        out_bias_grad.reshape(pools),
        loss.reshape(()),
    )


def solution(mesh):
    placed = (
        P("dp", None, "space", None),
        P("space", None),
        P("space", None),
        P(),
        P("dp", None, "space"),
        P(),
        P(),
        P(),
        P(),
        P(),
        P(),
    )
    return jax.shard_map(
        on_device,
        mesh=mesh,
        in_specs=placed,
        out_specs=(P("dp", None, "space"), P(), P(), P(), P(), P(), P(), P()),
        check_vma=False,
    )
```
